128 devices in a mesh: sec: 4 (over x_hi, core), dev: 32 (over z, y, x_lo).
Axes of the slice: x: 4 (x_hi: 2, x_lo: 2; x = x_hi * 2 + x_lo), y: 4, z: 4, core: 2. Of those that a mesh axis runs over, the one named last changes fastest.
Arguments:
- queries: bfloat16 [1024, 64, 576], P(('sec', 'dev')), may hold values from -6 to 6
- latent_cache: bfloat16 [1024, 1024, 576], P(('sec', 'dev')), may hold values from -9 to 9
- cache_length: int32 [1024], P(('sec', 'dev')), may hold values from 2 to 1024, as said below
- residual: bfloat16 [1024, 7168], P(('sec', 'dev')), may hold values from -9 to 9
- norm_gain: float32 [7168], replicated, may hold values from 0.1 to 1.9
- value_up: bfloat16 [64, 512, 128], P('dev'), may hold values from -4 to 4
- out_weight: bfloat16 [8192, 7168], P('dev'), may hold values from -0.0625 to 0.0625
- gate_weight: bfloat16 [7168, 8192], P(None, 'dev'), may hold values from -0.0625 to 0.0625
- up_weight: bfloat16 [7168, 8192], P(None, 'dev'), may hold values from -0.0625 to 0.0625
- down_weight: bfloat16 [8192, 7168], P('dev'), may hold values from -0.125 to 0.125
- expert_index: int32 [1024, 2], P(('sec', 'dev')), may hold values from 0 to 3, all different within a row; in each aligned block of 4 rows (0 to 3, 4 to 7, ...) at most 3 rows name the same one
- gate_level: int32 [1024, 2], P(('sec', 'dev')), may hold values from 1 to 4095
Outputs:
- layer_output: bfloat16 [1024, 7168], P(('sec', 'dev'))
The draws below stay inside these ranges and needn't reach their ends.
Inputs may be any that keep to these rules, and one draw needn't show every extreme that they name: `expert_index`: each token names 2 different experts. The rows of one device form 2 aligned blocks of 4 rows, and within such a block no expert is named more than 3 times. `cache_length`: some request of the first 3 sections holds exactly 1024 live positions.
All inputs are finite; a program needn't handle non-finite values.
Results may differ from the reference program's by a relative error of at most 0.03.
Values may be sent and summed in bfloat16 or wider, within the bound.
A program may use at most 192 MiB of HBM per device.

```python
import math
import jax
import jax.numpy as jnp
import numpy as np
from jax import lax

D = 7168
HEADS = 64
LAT = 512
ROPE = 64
VDIM = 128
FF = 2048
EXPERTS = 4
TOPK = 2
CACHE_LEN = 1024
KV = 576
MB_TOK = 4
CAP = 3
TOKENS = 1024
ATT_TOKENS = 768
N_DEV = 32


def draw_latent_cache(key, part):
    shape_all = (TOKENS, CACHE_LEN, KV)
    drawn = jnp.clip(jax.random.normal(jax.random.fold_in(key, 1), shape_all, jnp.float32), -4.0, 4.0)
    return drawn.astype(jnp.bfloat16)


def draw_queries(key, part):
    shape_all = (TOKENS, HEADS, KV)
    drawn = jnp.clip(jax.random.normal(jax.random.fold_in(key, 2), shape_all, jnp.float32), -4.0, 4.0)
    return drawn.astype(jnp.bfloat16)


def draw_cache_length(key, part):
    lengths = jax.random.randint(jax.random.fold_in(key, 3), (TOKENS,), 2, CACHE_LEN + 1)
    spot = jax.random.randint(jax.random.fold_in(key, 4), (), 0, ATT_TOKENS)
    return lengths.at[spot].set(CACHE_LEN).astype(jnp.int32)


def draw_residual(key, part):
    drawn = jnp.clip(jax.random.normal(jax.random.fold_in(key, 7), (TOKENS, D), jnp.float32), -4.0, 4.0)
    return drawn.astype(jnp.bfloat16)


def with_ends(values, key, low, top_value):
    longest = values.shape.index(max(values.shape))
    spots = []
    for shift in (0, 1):
        where = [jax.random.randint(jax.random.fold_in(key, axis), (), 0, length) for axis, length in enumerate(values.shape)]
        where[longest] = (where[longest] + shift) % values.shape[longest]
        spots.append(tuple(where))
    return values.at[spots[0]].set(low).at[spots[1]].set(top_value)


def block_scale(own_key, shape, split, low, top_value):
    factor_of, own = 1.0, jax.random.fold_in(own_key, 6)
    for position, parts in split:
        draws = jnp.exp(jax.random.uniform(jax.random.fold_in(own, position), (parts,), jnp.float32, low / len(split), top_value / len(split)))
        factor_of = factor_of * jnp.repeat(draws, shape[position] // parts).reshape([-1 if axis == position else 1 for axis in range(len(shape))])
    return factor_of


def shared_out(stream_key, own, number, rows, count, top, bound, lean):
    ranking = jax.random.permutation(stream_key, count)
    crowded, common = shares(count, rows * top, bound, lean, True), shares(count, rows * top, bound, lean, False)
    places = jnp.arange(count)

    def named(sizes, turn):
        used = int((sizes > 0).sum())
        fixed = max(1, used // 4)
        passed = fixed + (places - fixed + turn * (used - fixed)) % max(1, count - fixed)
        return jnp.zeros((count,), jnp.int32).at[ranking[jnp.where(places < fixed, places, passed)]].set(jnp.asarray(sizes, jnp.int32))

    sizes = jnp.where(number % 4 == 0, named(crowded, number // 4), named(common, number - number // 4 - 1))
    mixed = jax.random.permutation(jax.random.fold_in(own, 3), count)
    giver, taker = mixed[0:count // 2 * 2:2], mixed[1:count // 2 * 2:2]
    room = jnp.minimum(sizes[giver] - 1, bound - sizes[taker]) // 2
    room = jnp.where((giver == ranking[0]) | (taker == ranking[0]) | (sizes[taker] == 0), 0, jnp.maximum(room, 0))
    passed = jax.random.randint(jax.random.fold_in(own, 4), (count // 2,), 0, 1 << 20) % (room + 1)
    sizes = sizes.at[giver].add(-passed).at[taker].add(passed)
    items = jnp.searchsorted(jnp.cumsum(sizes), jnp.arange(rows * top), side="right").astype(jnp.int32)
    listing = items.reshape(top, rows).T
    listing = listing[jax.random.permutation(jax.random.fold_in(own, 1), rows)]
    turn = jax.random.randint(jax.random.fold_in(own, 2), (rows, 1), 0, top)
    return jnp.take_along_axis(listing, (jnp.arange(top)[None, :] + turn) % top, axis=1)


def shares(number_of, total, reach, lean, full):
    loads = [(1 << 20) // math.isqrt(standing ** lean) + 1 for standing in range(1, number_of + 1)]
    largest = reach if full else min(reach, max(-(-total // number_of), total * loads[0] // sum(loads)))
    least = 1 if total - largest >= number_of - 1 else 0
    holding, rest = [largest] + [least] * (number_of - 1), total - largest - least * (number_of - 1)
    while rest > 0:
        movable = [i for i in range(1, number_of) if holding[i] < largest] or [i for i in range(1, number_of) if holding[i] < reach]
        mass, left = sum([loads[i] for i in movable]), rest
        for i in movable:
            more = min(reach - holding[i], max(1, left * loads[i] // mass), rest)
            holding[i] = holding[i] + more
            rest = rest - more
    return np.array(holding)


def gaussian(stream_key, dims, width, bound, split=(), held_as=jnp.bfloat16):
    array = width * jax.random.normal(stream_key, dims, jnp.float32)
    if split:
        array = array * block_scale(stream_key, dims, split, -0.22, 0.18)
    return jnp.clip(array, -bound, bound).astype(held_as)


def setup_inputs(seed: int = 0) -> dict:
    keys = jax.random.split(jax.random.key(seed), 13)
    queries = draw_queries(jax.random.fold_in(keys[12], 71), 0)
    latent_cache = draw_latent_cache(jax.random.fold_in(keys[12], 71), 0)
    cache_length = draw_cache_length(jax.random.fold_in(keys[12], 71), 0)
    residual = draw_residual(jax.random.fold_in(keys[12], 71), 0)
    norm_gain = jnp.clip(1.0 + 0.18 * jax.random.normal(keys[4], (D,), jnp.float32), 0.1, 1.9)
    value_up = gaussian(keys[5], (HEADS, LAT, VDIM), 0.25, 4.0, ((0, 32),))
    out_weight = gaussian(keys[6], (HEADS * VDIM, D), (HEADS * VDIM) ** -0.5, 0.0625, ((0, 32),))
    gate_weight = gaussian(keys[7], (D, EXPERTS * FF), D ** -0.5, 0.0625, ((1, 32),))
    up_weight = gaussian(keys[8], (D, EXPERTS * FF), D ** -0.5, 0.0625, ((1, 32),))
    down_weight = gaussian(keys[9], (EXPERTS * FF, D), FF ** -0.5, 0.125, ((0, 32),))
    expert_index_keys = jax.random.split(jax.random.fold_in(keys[10], 1), TOKENS // MB_TOK)
    expert_index_turns = jax.random.permutation(jax.random.fold_in(keys[10], 3), TOKENS // MB_TOK)
    expert_index = jax.vmap(lambda own, number: shared_out(jax.random.fold_in(keys[10], 2), own, number, MB_TOK, EXPERTS, TOPK, CAP, 2))(expert_index_keys, expert_index_turns).reshape((TOKENS, TOPK))
    gate_level = with_ends(jax.random.randint(keys[11], (TOKENS, TOPK), 1, 4096), jax.random.fold_in(keys[11], 1), 1, 4095).astype(jnp.int32)
    return dict(queries=queries, latent_cache=latent_cache, cache_length=cache_length, residual=residual, norm_gain=norm_gain, value_up=value_up, out_weight=out_weight, gate_weight=gate_weight, up_weight=up_weight, down_weight=down_weight, expert_index=expert_index, gate_level=gate_level)


def reference(queries, latent_cache, cache_length, residual, norm_gain, value_up, out_weight, gate_weight, up_weight, down_weight, expert_index, gate_level):
    active = ATT_TOKENS
    score_scale = (VDIM + ROPE) ** (-0.5)
    positions = jnp.arange(CACHE_LEN, dtype=jnp.int32)
    value_float = value_up.astype(jnp.float32)

    def attend(item):
        query_one, cache_one, length_one = item
        scores = jnp.dot(query_one, cache_one.T, preferred_element_type=jnp.float32) * score_scale
        usable = positions[None, :] < length_one
        masked = jnp.where(usable, scores, -1e+30)
        highest = lax.optimization_barrier(jnp.max(masked, axis=1, keepdims=True))
        expos = jnp.where(usable, jnp.exp(masked - highest), 0.0)
        weights = (expos / lax.optimization_barrier(jnp.sum(expos, axis=1, keepdims=True))).astype(jnp.bfloat16)
        latent_out = jnp.dot(weights, cache_one, preferred_element_type=jnp.float32)[:, :LAT].astype(jnp.bfloat16)
        head_out = jnp.einsum('hc,hcv->hv', latent_out.astype(jnp.float32), value_float).astype(jnp.bfloat16)
        return jnp.dot(head_out.reshape(1, HEADS * VDIM), out_weight, preferred_element_type=jnp.float32)[0]
    attended = lax.map(attend, (queries[:active], latent_cache[:active], cache_length[:active]))
    stream = (residual[:active].astype(jnp.float32) + attended).astype(jnp.bfloat16)
    stream_float = stream.astype(jnp.float32)
    mean_square = lax.optimization_barrier(jnp.mean(stream_float * stream_float, axis=1, keepdims=True))
    normed = (stream_float * lax.rsqrt(mean_square + 1e-06) * norm_gain).astype(jnp.bfloat16)
    levels = gate_level[:active].astype(jnp.float32)
    mix = levels / lax.optimization_barrier(jnp.sum(levels, axis=1, keepdims=True))
    chosen = expert_index[:active]
    slab_count = N_DEV // EXPERTS
    slab_width = FF // slab_count
    moe = jnp.zeros((active, D), jnp.float32)
    for expert in range(EXPERTS):
        gate_hidden = jnp.dot(normed, gate_weight[:, expert * FF:(expert + 1) * FF], preferred_element_type=jnp.float32)
        up_hidden = jnp.dot(normed, up_weight[:, expert * FF:(expert + 1) * FF], preferred_element_type=jnp.float32)
        activated = (jax.nn.silu(gate_hidden) * up_hidden).astype(jnp.bfloat16).reshape(active, slab_count, slab_width)
        down_slabs = down_weight[expert * FF:(expert + 1) * FF].reshape(slab_count, slab_width, D)
        partial_out = jnp.einsum('tsf,sfd->tsd', activated.astype(jnp.float32), down_slabs.astype(jnp.float32)).astype(jnp.bfloat16)
        slab_total = lax.optimization_barrier(jnp.sum(partial_out.astype(jnp.float32), axis=1))
        weight_of = lax.optimization_barrier(jnp.sum(jnp.where(chosen == expert, mix, 0.0), axis=1))
        moe = moe + weight_of[:, None] * slab_total
    result = (stream_float + moe).astype(jnp.bfloat16)
    rest_rows = jnp.zeros((TOKENS - active, D), jnp.bfloat16)
    return jnp.concatenate([result, rest_rows], axis=0)
```

```python
import functools

import jax
import jax.numpy as jnp
from jax import lax
from jax.experimental import pallas as pl
from jax.experimental.pallas import tpu as pltpu
from jax.sharding import PartitionSpec as P

EXPERTS = 4
TOPK = 2
ROWS = 8
GROUP = 32
DIMS = 5
TILE = 256
MASKS = (1, 2, 6, 8, 24)
STEP_AT = (0, 16, 24, 28, 30)
MESH = pl.DeviceIdType.MESH


def mask_of(code):
    mask = 0
    for dim in range(DIMS):
        if (code >> dim) & 1:
            mask ^= MASKS[dim]
    return mask


def order_of(chunk):
    return [(chunk + step) % DIMS for step in range(DIMS)]


def place_of(chunk, code):
    place = 0
    for step, dim in enumerate(order_of(chunk)):
        place += ((code >> dim) & 1) << (DIMS - 1 - step)
    return place


def flipped(bits, mask):
    total = 0
    for i, bit in enumerate(bits):
        total = total + (1 << i) * ((1 - bit) if (mask >> i) & 1 else bit)
    return total


def layer_kernel(
    widths,
    head_ref,
    residual_ref,
    gain_ref,
    share_ref,
    out_weight_hbm,
    gate_hbm,
    up_hbm,
    down_hbm,
    out_ref,
    out_weight,
    gate,
    up,
    down,
    wide,
    left,
    stream,
    gate_sum,
    up_sum,
    act,
    load_sem,
    send_sem,
    recv_sem,
    *buffers,
):
    chunks = len(widths)
    partial = buffers[:chunks]
    landing = buffers[chunks : 2 * chunks]
    landing_two = buffers[2 * chunks : 3 * chunks]
    rows_of = buffers[3 * chunks :]
    starts = [sum(widths[:k]) for k in range(chunks)]
    section = lax.axis_index("sec")
    me = lax.axis_index("dev")
    bits = [(me // (1 << i)) % 2 for i in range(DIMS)]
    partners = [flipped(bits, mask) for mask in MASKS]

    loads = []
    for i, (source, target) in enumerate(
        ((out_weight_hbm, out_weight), (gate_hbm, gate), (up_hbm, up), (down_hbm, down))
    ):
        load = pltpu.make_async_copy(source, target, load_sem.at[i])
        load.start()
        loads.append(load)

    barrier = pltpu.get_barrier_semaphore()
    for partner in partners:
        pl.semaphore_signal(barrier, inc=1, device_id=(section, partner), device_id_type=MESH)
    pl.semaphore_wait(barrier, DIMS)

    def send(source, target, phase, chunk, step, dim):
        copy = pltpu.make_async_remote_copy(
            src_ref=source,
            dst_ref=target,
            send_sem=send_sem.at[phase, chunk, step],
            recv_sem=recv_sem.at[phase, chunk, step],
            device_id=(section, partners[dim]),
            device_id_type=MESH,
        )
        copy.start()
        return copy

    def reduce_send(phase, chunk, step, arrivals):
        half = 16 >> step
        return send(
            partial[chunk].at[pl.ds(half, half)],
            arrivals[chunk].at[pl.ds(STEP_AT[step], half)],
            phase,
            chunk,
            step,
            order_of(chunk)[step],
        )

    def add_rows(chunk, arrivals, at, first, count):
        @pl.loop(0, count)
        def _(i):
            row = first + i
            partial[chunk][row] = partial[chunk][row] + arrivals[chunk][at + row]

    def reduce_scatter(phase, copies, arrivals):
        started = list(copies)
        current = list(copies)
        for step in range(DIMS):
            half = 16 >> step
            for chunk in range(chunks):
                current[chunk].wait_recv()
                if step < DIMS - 1:
                    add_rows(chunk, arrivals, STEP_AT[step], half // 2, half // 2)
                    current[chunk] = reduce_send(phase, chunk, step + 1, arrivals)
                    started.append(current[chunk])
                    add_rows(chunk, arrivals, STEP_AT[step], 0, half // 2)
                else:
                    add_rows(chunk, arrivals, STEP_AT[step], 0, 1)
        return started

    def project(chunk, operand, weight, scale):
        @pl.loop(0, widths[chunk] // TILE)
        def _(i):
            inner = pl.ds(pl.multiple_of(i * TILE, TILE), TILE)
            outer = pl.ds(pl.multiple_of(starts[chunk] + i * TILE, TILE), TILE)
            product = jnp.dot(operand[...], weight[:, outer], preferred_element_type=jnp.float32)
            if scale is not None:
                product = product * scale
            for code in range(GROUP):
                block = product[code * ROWS : (code + 1) * ROWS]
                partial[chunk][place_of(chunk, code), :, inner] = block.astype(jnp.bfloat16)

    for code in range(GROUP):
        block = head_ref[flipped(bits, mask_of(code))].astype(jnp.float32)
        wide[code * ROWS : (code + 1) * ROWS] = block
    left[...] = wide[...].astype(jnp.bfloat16)
    loads[0].wait()
    copies = []
    for chunk in range(chunks):
        project(chunk, left, out_weight, None)
        copies.append(reduce_send(0, chunk, 0, landing))
    started = reduce_scatter(0, copies, landing)

    square = jnp.zeros((ROWS, 1), jnp.float32)
    for chunk in range(chunks):
        columns = pl.ds(starts[chunk], widths[chunk])
        attended = partial[chunk][0].astype(jnp.float32)
        total = (residual_ref[:, columns].astype(jnp.float32) + attended).astype(jnp.bfloat16)
        stream[:, columns] = total
        total = total.astype(jnp.float32)
        square = square + jnp.sum(total * total, axis=1, keepdims=True)
    level = lax.rsqrt(square / stream.shape[1] + 1e-06)
    gathers = [[] for _ in range(chunks)]

    def gather_send(chunk, step):
        count = 1 << step
        copy = send(
            rows_of[chunk].at[pl.ds(0, count)],
            rows_of[chunk].at[pl.ds(count, count)],
            1,
            chunk,
            step,
            order_of(chunk)[DIMS - 1 - step],
        )
        gathers[chunk].append(copy)

    for chunk in range(chunks):
        columns = pl.ds(starts[chunk], widths[chunk])
        normed = stream[:, columns].astype(jnp.float32) * level * gain_ref[:, columns]
        rows_of[chunk][0, :, : widths[chunk]] = normed.astype(jnp.bfloat16)
        if chunk == chunks - 1:
            rows_of[chunk][0, :, widths[chunk] :] = share_ref[...]
        gather_send(chunk, 0)
    for step in range(1, DIMS):
        for chunk in range(chunks):
            gathers[chunk][step - 1].wait_recv()
            gather_send(chunk, step)
    gate_sum[...] = jnp.zeros_like(gate_sum)
    up_sum[...] = jnp.zeros_like(up_sum)
    loads[1].wait()
    loads[2].wait()

    def stacked(chunk, columns):
        blocks = [
            rows_of[chunk][place_of(chunk, code), :, columns].astype(jnp.float32)
            for code in range(GROUP)
        ]
        return jnp.concatenate(blocks, axis=0)

    for chunk in range(chunks):
        gathers[chunk][DIMS - 1].wait_recv()

        @pl.loop(0, widths[chunk] // TILE)
        def _(i):
            inner = pl.ds(pl.multiple_of(i * TILE, TILE), TILE)
            outer = pl.ds(pl.multiple_of(starts[chunk] + i * TILE, TILE), TILE)
            rows = stacked(chunk, inner).astype(jnp.bfloat16)
            gate_sum[...] += jnp.dot(rows, gate[outer, :], preferred_element_type=jnp.float32)
            up_sum[...] += jnp.dot(rows, up[outer, :], preferred_element_type=jnp.float32)

    shares = stacked(chunks - 1, pl.ds(widths[chunks - 1], 128))
    lane = lax.broadcasted_iota(jnp.int32, shares.shape, 1)
    expert = me // (GROUP // EXPERTS)
    share = jnp.sum(
        jnp.where((lane == expert) | (lane == expert + EXPERTS), shares, 0.0), axis=1, keepdims=True
    )
    hidden = gate_sum[...]
    act[...] = (hidden / (1.0 + jnp.exp(-hidden)) * up_sum[...]).astype(jnp.bfloat16)
    loads[3].wait()
    for copy in started:
        copy.wait_send()
    copies = []
    for chunk in range(chunks):
        project(chunk, act, down, share)
        copies.append(reduce_send(2, chunk, 0, landing_two))
    started = reduce_scatter(2, copies, landing_two)
    for chunk in range(chunks):
        columns = pl.ds(starts[chunk], widths[chunk])
        result = stream[:, columns].astype(jnp.float32) + partial[chunk][0].astype(jnp.float32)
        result = jnp.where(section < lax.axis_size("sec") - 1, result, 0.0)
        out_ref[:, columns] = result.astype(jnp.bfloat16)
    for chunk in range(chunks):
        for copy in gathers[chunk]:
            copy.wait_send()
    for copy in started:
        copy.wait_send()


def layer_tail(heads, residual, gain, shares, out_weight, gate_weight, up_weight, down_weight):
    width = residual.shape[1]
    tiles = width // TILE
    widths = [TILE * (tiles // DIMS + (1 if k < tiles % DIMS else 0)) for k in range(DIMS)]
    hidden = gate_weight.shape[1]
    bf16, f32 = jnp.bfloat16, jnp.float32
    vmem = pl.BlockSpec(memory_space=pltpu.VMEM)
    hbm = pl.BlockSpec(memory_space=pl.ANY)
    scratch = [
        pltpu.VMEM(out_weight.shape, bf16),
        pltpu.VMEM(gate_weight.shape, bf16),
        pltpu.VMEM(up_weight.shape, bf16),
        pltpu.VMEM(down_weight.shape, bf16),
        pltpu.VMEM((GROUP * ROWS, heads.shape[2]), f32),
        pltpu.VMEM((GROUP * ROWS, heads.shape[2]), bf16),
        pltpu.VMEM((ROWS, width), bf16),
        pltpu.VMEM((GROUP * ROWS, hidden), f32),
        pltpu.VMEM((GROUP * ROWS, hidden), f32),
        pltpu.VMEM((GROUP * ROWS, hidden), bf16),
        pltpu.SemaphoreType.DMA((4,)),
        pltpu.SemaphoreType.DMA((3, DIMS, DIMS)),
        pltpu.SemaphoreType.DMA((3, DIMS, DIMS)),
    ]
    scratch += [pltpu.VMEM((GROUP, ROWS, w), bf16) for w in widths]
    scratch += [pltpu.VMEM((GROUP - 1, ROWS, w), bf16) for w in widths] * 2
    extra = [0] * (DIMS - 1) + [128]
    scratch += [pltpu.VMEM((GROUP, ROWS, w + e), bf16) for w, e in zip(widths, extra)]
    return pl.pallas_call(
        functools.partial(layer_kernel, widths),
        out_shape=jax.ShapeDtypeStruct(residual.shape, bf16),
        in_specs=[vmem] * 4 + [hbm] * 4,
        out_specs=vmem,
        scratch_shapes=scratch,
        compiler_params=pltpu.CompilerParams(
            collective_id=0, has_side_effects=True, vmem_limit_bytes=56 * 1024 * 1024
        ),
    )(heads, residual, gain, shares, out_weight, gate_weight, up_weight, down_weight)


def body(
    queries,
    latent_cache,
    cache_length,
    residual,
    norm_gain,
    value_up,
    out_weight,
    gate_weight,
    up_weight,
    down_weight,
    expert_index,
    gate_level,
):
    latent_width = value_up.shape[1]
    score_scale = (value_up.shape[2] + queries.shape[2] - latent_width) ** (-0.5)
    scores = (
        jnp.einsum("thc,tpc->thp", queries, latent_cache, preferred_element_type=jnp.float32)
        * score_scale
    )
    position = lax.broadcasted_iota(jnp.int32, (1, 1, latent_cache.shape[1]), 2)
    usable = position < cache_length[:, None, None]
    masked = jnp.where(usable, scores, -1e30)
    highest = jnp.max(masked, axis=2, keepdims=True)
    expos = jnp.where(usable, jnp.exp(masked - highest), 0.0)
    weights = (expos / jnp.sum(expos, axis=2, keepdims=True)).astype(jnp.bfloat16)
    latent_out = jnp.einsum(
        "thp,tpc->thc", weights, latent_cache, preferred_element_type=jnp.float32
    )[:, :, :latent_width].astype(jnp.bfloat16)
    by_heads = lax.all_to_all(latent_out, "dev", split_axis=1, concat_axis=0, tiled=True)
    head_out = jnp.einsum(
        "thc,hcv->thv", by_heads, value_up, preferred_element_type=jnp.float32
    ).astype(jnp.bfloat16)
    heads = head_out.reshape(GROUP, ROWS, -1)

    levels = gate_level.astype(jnp.float32)
    mix = levels / jnp.sum(levels, axis=1, keepdims=True)
    named = expert_index[:, :, None] == jnp.arange(EXPERTS, dtype=jnp.int32)[None, None, :]
    share = jnp.sum(jnp.where(named, mix[:, :, None], 0.0), axis=1)
    coarse = share.astype(jnp.bfloat16)
    fine = (share - coarse.astype(jnp.float32)).astype(jnp.bfloat16)
    shares = jnp.pad(jnp.concatenate([coarse, fine], axis=1), ((0, 0), (0, 128 - 2 * EXPERTS)))
    return layer_tail(
        heads,
        residual,
        norm_gain.reshape(1, -1),
        shares,
        out_weight,
        gate_weight,
        up_weight,
        down_weight,
    )


def solution(mesh):
    placed = (
        P(("sec", "dev"), None, None),
        P(("sec", "dev"), None, None),
        P(("sec", "dev")),
        P(("sec", "dev"), None),
        P(),
        P("dev", None, None),
        P("dev", None),
        P(None, "dev"),
        P(None, "dev"),
        P("dev", None),
        P(("sec", "dev"), None),
        P(("sec", "dev"), None),
    )
    return jax.shard_map(
        body, mesh=mesh, in_specs=placed, out_specs=P(("sec", "dev"), None), check_vma=False
    )
```

```python
import functools

import jax
import jax.numpy as jnp
from jax import lax
from jax.experimental import pallas as pl
from jax.experimental.pallas import tpu as pltpu
from jax.sharding import PartitionSpec as P

EXPERTS = 4
TOPK = 2
ROWS = 8
GROUP = 32
DIMS = 5
TILE = 256
LANES = 128
CHUNKS = 8
SPREAD = 4
SLOTS = 2 * SPREAD + 3
MASKS = (1, 2, 6, 8, 24)
MESH = pl.DeviceIdType.MESH


def mask_of(code):
    mask = 0
    for dim in range(DIMS):
        if (code >> dim) & 1:
            mask ^= MASKS[dim]
    return mask


def flipped(bits, mask):
    total = 0
    for i, bit in enumerate(bits):
        total = total + (1 << i) * ((1 - bit) if (mask >> i) & 1 else bit)
    return total


class Plan:
    def __init__(self, core):
        self.core = core
        self.blocks = GROUP if core == 0 else GROUP // 2
        self.halvings = 3 if core == 0 else 2
        self.rows = self.blocks * ROWS

    def order(self, chunk):
        turn = chunk // 2 if self.core == 0 else chunk
        ring = [1 + (turn + i) % 4 for i in range(4)]
        if self.core == 1:
            return ring
        return [0] + ring if chunk % 2 == 0 else ring + [0]

    def codes(self):
        return [(code if self.core == 0 else 2 * code) for code in range(self.blocks)]

    def place(self, chunk, code):
        order = self.order(chunk)
        place = 0
        for step, dim in enumerate(order):
            place += ((code >> dim) & 1) << (len(order) - 1 - step)
        return place

    def code(self, chunk, place):
        order = self.order(chunk)
        code = 0
        for step, dim in enumerate(order):
            code += ((place >> (len(order) - 1 - step)) & 1) << dim
        return code


def work(plan, widths, refs, buffers, loads):
    (
        latent_ref,
        residual_ref,
        gain_ref,
        share_ref,
        value_ref,
        out_ref,
        out_weight,
        gate,
        up,
        down,
        latents,
        left,
        stream,
        gate_sum,
        up_sum,
        act,
        pass_send,
        pass_recv,
        send_sem,
        recv_sem,
    ) = refs
    partial = buffers[:CHUNKS]
    landings = (buffers[CHUNKS : 2 * CHUNKS], None, buffers[2 * CHUNKS : 3 * CHUNKS])
    rows_of = buffers[3 * CHUNKS :]
    starts = [sum(widths[:k]) for k in range(CHUNKS)]
    section = lax.axis_index("sec")
    me = lax.axis_index("dev")
    bits = [(me // (1 << i)) % 2 for i in range(DIMS)]
    devices = {code: flipped(bits, mask_of(code)) for code in range(GROUP)}
    across = lax.rem(section + 2, 4)
    blocks, rows, halvings = plan.blocks, plan.rows, plan.halvings
    base = pl.ds(0, rows)
    owning = section < 3

    def peer(code):
        return (across if plan.core == 1 and code % 2 else section, devices[code])

    def when_owning(owns, run):
        if plan.core == 0:
            if owns:
                run()
        else:
            pl.when(owning if owns else jnp.logical_not(owning))(run)

    barrier = pltpu.get_barrier_semaphore()
    for code in range(1, GROUP):
        pl.semaphore_signal(barrier, inc=1, device_id=peer(code), device_id_type=MESH)
    pl.semaphore_wait(barrier, GROUP - 1)

    def passing(code):
        slot = code if plan.core == 0 else code // 2
        return pltpu.make_async_remote_copy(
            src_ref=latent_ref.at[devices[code]],
            dst_ref=latents.at[slot],
            send_sem=pass_send.at[code],
            recv_sem=pass_recv.at[slot],
            device_id=peer(code),
            device_id_type=MESH,
        )

    def pass_out():
        for code in range(1, GROUP):
            passing(code).start()
        latents[0] = latent_ref[me]

    def pass_in(codes):
        for code in codes:
            passing(code).wait_recv()

    when_owning(True, pass_out)
    if plan.core == 0:
        pass_in(range(1, GROUP))
    else:
        when_owning(True, lambda: pass_in(range(2, GROUP, 2)))
        when_owning(False, lambda: pass_in(range(1, GROUP, 2)))
    for head in range(2):
        lines = latents[pl.ds(0, blocks), head * ROWS : (head + 1) * ROWS, :].astype(jnp.float32)
        lines = lines.reshape(rows, lines.shape[2]).astype(jnp.bfloat16)
        valued = jnp.dot(lines, value_ref[head], preferred_element_type=jnp.float32)
        left[base, head * LANES : (head + 1) * LANES] = valued.astype(jnp.bfloat16)

    started = []

    def copy_of(source, target, phase, chunk, slot, out_slot, code):
        return pltpu.make_async_remote_copy(
            src_ref=source,
            dst_ref=target,
            send_sem=send_sem.at[phase, chunk, out_slot],
            recv_sem=recv_sem.at[phase, chunk, slot],
            device_id=peer(code),
            device_id_type=MESH,
        )

    def go(copy):
        copy.start()
        started.append(copy)
        return copy

    def halving(phase, chunk, step):
        half = (blocks // 2) >> step
        places = pl.ds(half, half)
        slot = 2 * SPREAD + step
        return copy_of(
            partial[chunk].at[places],
            landings[phase][chunk].at[places],
            phase,
            chunk,
            slot,
            slot,
            1 << plan.order(chunk)[step],
        )

    def direct(phase, chunk, place):
        return copy_of(
            partial[chunk].at[place],
            landings[phase][chunk].at[place],
            phase,
            chunk,
            place,
            place,
            plan.code(chunk, place),
        )

    def direct_across(phase, chunk, place):
        return copy_of(
            partial[chunk].at[place],
            landings[phase][chunk].at[16 + place],
            phase,
            chunk,
            SPREAD + place,
            SPREAD + place,
            plan.code(chunk, place) + 1,
        )

    def sum_send(phase, chunk, step):
        if step < halvings:
            go(halving(phase, chunk, step))
            return

        def to_owners():
            for place in range(1, SPREAD):
                direct(phase, chunk, place).start()

        def to_owners_across():
            for place in range(SPREAD):
                direct_across(phase, chunk, place).start()

        when_owning(True, to_owners)
        when_owning(False, to_owners_across)

    def sum_sent(phase):
        def to_owners():
            for chunk in range(CHUNKS):
                for place in range(1, SPREAD):
                    direct(phase, chunk, place).wait_send()

        def to_owners_across():
            for chunk in range(CHUNKS):
                for place in range(SPREAD):
                    direct_across(phase, chunk, place).wait_send()

        when_owning(True, to_owners)
        when_owning(False, to_owners_across)

    def all_sent():
        for copy in started:
            copy.wait_send()
        del started[:]

    def add_rows(phase, chunk, half, first, count):
        @pl.loop(0, count)
        def _(i):
            row = first + i
            partial[chunk][row] = partial[chunk][row] + landings[phase][chunk][half + row]

    def sum_step(phase, chunk, step):
        half = (blocks // 2) >> step
        halving(phase, chunk, step).wait_recv()
        ahead = half // 2 if step < halvings - 1 else 0
        add_rows(phase, chunk, half, ahead, half - ahead)
        sum_send(phase, chunk, step + 1)
        if ahead:
            add_rows(phase, chunk, half, 0, ahead)

    def sum_last(phase, chunk):
        total = partial[chunk][0].astype(jnp.float32)
        for place in range(1, SPREAD):
            direct(phase, chunk, place).wait_recv()
            total = total + landings[phase][chunk][place].astype(jnp.float32)
        if plan.core == 1:
            for place in range(SPREAD):
                direct_across(phase, chunk, place).wait_recv()
                total = total + landings[phase][chunk][16 + place].astype(jnp.float32)
        return total

    def tiled(chunk, one):
        whole = widths[chunk] // TILE

        @pl.loop(0, whole)
        def _(i):
            one(pl.multiple_of(i * TILE, TILE), TILE)

        if widths[chunk] % TILE:
            one(whole * TILE, widths[chunk] % TILE)

    def project(chunk, operand, weight, scale):
        def one(offset, size):
            inner = pl.ds(offset, size)
            outer = pl.ds(pl.multiple_of(starts[chunk] + offset, LANES), size)
            product = jnp.dot(
                operand[base, :], weight[:, outer], preferred_element_type=jnp.float32
            )
            if scale is not None:
                product = product * scale
            for i, code in enumerate(plan.codes()):
                block = product[i * ROWS : (i + 1) * ROWS]
                partial[chunk][plan.place(chunk, code), :, inner] = block.astype(jnp.bfloat16)

        tiled(chunk, one)

    loads[0].wait()
    for chunk in range(CHUNKS):
        project(chunk, left, out_weight, None)
        sum_send(0, chunk, 0)
    for step in range(halvings):
        for chunk in range(CHUNKS):
            sum_step(0, chunk, step)

    def gather_near(chunk, place):
        return copy_of(
            rows_of[chunk].at[0],
            rows_of[chunk].at[place],
            1,
            chunk,
            place,
            place,
            plan.code(chunk, place),
        )

    def gather_across(chunk, place):
        return copy_of(
            rows_of[chunk].at[0],
            rows_of[chunk].at[place],
            1,
            chunk,
            place,
            SPREAD + place,
            plan.code(chunk, place) + 1,
        )

    def doubling(chunk, step):
        count = (blocks // 2) >> step
        slot = 2 * SPREAD + step
        return copy_of(
            rows_of[chunk].at[pl.ds(0, count)],
            rows_of[chunk].at[pl.ds(count, count)],
            1,
            chunk,
            slot,
            slot,
            1 << plan.order(chunk)[step],
        )

    def attended_rows():
        square = jnp.zeros((ROWS, 1), jnp.float32)
        for chunk in range(CHUNKS):
            columns = pl.ds(starts[chunk], widths[chunk])
            total = residual_ref[:, columns].astype(jnp.float32) + sum_last(0, chunk)
            total = total.astype(jnp.bfloat16)
            stream[:, columns] = total
            total = total.astype(jnp.float32)
            square = square + jnp.sum(total * total, axis=1, keepdims=True)
            scaled = total * gain_ref[:, columns]
            rows_of[chunk][0, :, : widths[chunk]] = scaled.astype(jnp.bfloat16)
            if chunk == CHUNKS - 1:
                level = lax.rsqrt(square / stream.shape[1] + 1e-06)
                coarse = level.astype(jnp.bfloat16).astype(jnp.float32)
                lane = lax.broadcasted_iota(jnp.int32, (ROWS, LANES), 1)
                extra = share_ref[...].astype(jnp.float32)
                extra = jnp.where(lane == 2 * EXPERTS, coarse, extra)
                extra = jnp.where(lane == 2 * EXPERTS + 1, level - coarse, extra)
                rows_of[chunk][0, :, widths[chunk] :] = extra.astype(jnp.bfloat16)
            for place in range(SPREAD):
                if place:
                    gather_near(chunk, place).start()
                if plan.core == 1:
                    gather_across(chunk, place).start()

    when_owning(True, attended_rows)
    for step in reversed(range(halvings)):
        for chunk in range(CHUNKS):
            if step == halvings - 1:
                when_owning(False, lambda: gather_across(chunk, 0).wait_recv())
                for place in range(1, SPREAD):
                    gather_near(chunk, place).wait_recv()
            else:
                doubling(chunk, step + 1).wait_recv()
            go(doubling(chunk, step))
    gate_sum[base, :] = jnp.zeros((rows, gate_sum.shape[1]), jnp.float32)
    up_sum[base, :] = jnp.zeros((rows, up_sum.shape[1]), jnp.float32)
    loads[1].wait()
    loads[2].wait()

    def stacked(chunk, columns):
        lines = [
            rows_of[chunk][plan.place(chunk, code), :, columns].astype(jnp.float32)
            for code in plan.codes()
        ]
        return jnp.concatenate(lines, axis=0)

    for chunk in range(CHUNKS):
        doubling(chunk, 0).wait_recv()

        def one(offset, size):
            outer = pl.ds(pl.multiple_of(starts[chunk] + offset, LANES), size)
            lines = stacked(chunk, pl.ds(offset, size)).astype(jnp.bfloat16)
            gate_sum[base, :] += jnp.dot(lines, gate[outer, :], preferred_element_type=jnp.float32)
            up_sum[base, :] += jnp.dot(lines, up[outer, :], preferred_element_type=jnp.float32)

        tiled(chunk, one)

    shares = stacked(CHUNKS - 1, pl.ds(widths[CHUNKS - 1], LANES))
    lane = lax.broadcasted_iota(jnp.int32, shares.shape, 1)
    expert = me // (GROUP // EXPERTS)

    def picked(first, second):
        chosen = (lane == first) | (lane == second)
        return jnp.sum(jnp.where(chosen, shares, 0.0), axis=1, keepdims=True)

    share = picked(expert, expert + EXPERTS)
    level = picked(2 * EXPERTS, 2 * EXPERTS + 1)
    hidden = gate_sum[base, :] * level
    hidden = hidden / (1.0 + jnp.exp(-hidden)) * (up_sum[base, :] * level)
    act[base, :] = hidden.astype(jnp.bfloat16)
    loads[3].wait()
    all_sent()
    sum_sent(0)
    for chunk in range(CHUNKS):
        project(chunk, act, down, share)
        sum_send(2, chunk, 0)
    for step in range(halvings):
        for chunk in range(CHUNKS):
            sum_step(2, chunk, step)

    def finish():
        for chunk in range(CHUNKS):
            columns = pl.ds(starts[chunk], widths[chunk])
            result = stream[:, columns].astype(jnp.float32) + sum_last(2, chunk)
            out_ref[:, columns] = result.astype(jnp.bfloat16)
        for code in range(1, GROUP):
            passing(code).wait_send()
        for chunk in range(CHUNKS):
            for place in range(SPREAD):
                if place:
                    gather_near(chunk, place).wait_send()
                if plan.core == 1:
                    gather_across(chunk, place).wait_send()

    def blank():
        out_ref[...] = jnp.zeros_like(out_ref)

    when_owning(True, finish)
    when_owning(False, blank)
    all_sent()
    sum_sent(2)


def layer_kernel(
    widths,
    latent_ref,
    residual_ref,
    gain_ref,
    share_ref,
    value_ref,
    out_weight_hbm,
    gate_hbm,
    up_hbm,
    down_hbm,
    out_ref,
    out_weight,
    gate,
    up,
    down,
    latents,
    left,
    stream,
    gate_sum,
    up_sum,
    act,
    load_sem,
    pass_send,
    pass_recv,
    send_sem,
    recv_sem,
    *buffers,
):
    loads = []
    for i, (source, target) in enumerate(
        ((out_weight_hbm, out_weight), (gate_hbm, gate), (up_hbm, up), (down_hbm, down))
    ):
        load = pltpu.make_async_copy(source, target, load_sem.at[i])
        load.start()
        loads.append(load)
    refs = (latent_ref, residual_ref, gain_ref, share_ref, value_ref, out_ref)
    refs += (out_weight, gate, up, down, latents, left, stream, gate_sum, up_sum, act)
    refs += (pass_send, pass_recv, send_sem, recv_sem)
    core = lax.axis_index("sec") % 2
    for number in range(2):
        pl.when(core == number)(
            functools.partial(work, Plan(number), widths, refs, buffers, loads)
        )


def chunk_widths(width):
    units = width // LANES
    return [LANES * (units // CHUNKS + (1 if k < units % CHUNKS else 0)) for k in range(CHUNKS)]


def layer_tail(latents, residual, gain, shares, value_up, *weights):
    width = residual.shape[1]
    widths = chunk_widths(width)
    hidden = weights[1].shape[1]
    bf16, f32 = jnp.bfloat16, jnp.float32
    vmem = pl.BlockSpec(memory_space=pltpu.VMEM)
    hbm = pl.BlockSpec(memory_space=pl.ANY)
    scratch = [pltpu.VMEM(weight.shape, bf16) for weight in weights]
    scratch += [
        pltpu.VMEM(latents.shape, bf16),
        pltpu.VMEM((GROUP * ROWS, 2 * LANES), bf16),
        pltpu.VMEM((ROWS, width), bf16),
        pltpu.VMEM((GROUP * ROWS, hidden), f32),
        pltpu.VMEM((GROUP * ROWS, hidden), f32),
        pltpu.VMEM((GROUP * ROWS, hidden), bf16),
        pltpu.SemaphoreType.DMA((4,)),
        pltpu.SemaphoreType.DMA((GROUP,)),
        pltpu.SemaphoreType.DMA((GROUP,)),
        pltpu.SemaphoreType.DMA((3, CHUNKS, SLOTS)),
        pltpu.SemaphoreType.DMA((3, CHUNKS, SLOTS)),
    ]
    scratch += [pltpu.VMEM((GROUP, ROWS, w), bf16) for w in widths] * 3
    extra = [0] * (CHUNKS - 1) + [LANES]
    scratch += [pltpu.VMEM((GROUP, ROWS, w + e), bf16) for w, e in zip(widths, extra)]
    return pl.pallas_call(
        functools.partial(layer_kernel, widths),
        out_shape=jax.ShapeDtypeStruct(residual.shape, bf16),
        in_specs=[vmem] * 5 + [hbm] * 4,
        out_specs=vmem,
        scratch_shapes=scratch,
        compiler_params=pltpu.CompilerParams(
            collective_id=0, has_side_effects=True, vmem_limit_bytes=56 * 1024 * 1024
        ),
    )(latents, residual, gain, shares, value_up, *weights)


def body(
    queries,
    latent_cache,
    cache_length,
    residual,
    norm_gain,
    value_up,
    out_weight,
    gate_weight,
    up_weight,
    down_weight,
    expert_index,
    gate_level,
):
    latent_width = value_up.shape[1]
    score_scale = (value_up.shape[2] + queries.shape[2] - latent_width) ** (-0.5)
    scores = (
        jnp.einsum("thc,tpc->thp", queries, latent_cache, preferred_element_type=jnp.float32)
        * score_scale
    )
    position = lax.broadcasted_iota(jnp.int32, (1, 1, latent_cache.shape[1]), 2)
    usable = position < cache_length[:, None, None]
    masked = jnp.where(usable, scores, -1e30)
    highest = jnp.max(masked, axis=2, keepdims=True)
    expos = jnp.where(usable, jnp.exp(masked - highest), 0.0)
    weights = (expos / jnp.sum(expos, axis=2, keepdims=True)).astype(jnp.bfloat16)
    latent_out = jnp.einsum(
        "thp,tpc->thc", weights, latent_cache, preferred_element_type=jnp.float32
    )[:, :, :latent_width].astype(jnp.bfloat16)
    tokens, heads = latent_out.shape[:2]
    latents = jnp.swapaxes(latent_out, 0, 1).reshape(GROUP, heads // GROUP * tokens, latent_width)

    levels = gate_level.astype(jnp.float32)
    mix = levels / jnp.sum(levels, axis=1, keepdims=True)
    named = expert_index[:, :, None] == jnp.arange(EXPERTS, dtype=jnp.int32)[None, None, :]
    share = jnp.sum(jnp.where(named, mix[:, :, None], 0.0), axis=1)
    coarse = share.astype(jnp.bfloat16)
    fine = (share - coarse.astype(jnp.float32)).astype(jnp.bfloat16)
    shares = jnp.pad(jnp.concatenate([coarse, fine], axis=1), ((0, 0), (0, 128 - 2 * EXPERTS)))
    return layer_tail(
        latents,
        residual,
        norm_gain.reshape(1, -1),
        shares,
        value_up,
        out_weight,
        gate_weight,
        up_weight,
        down_weight,
    )


def solution(mesh):
    placed = (
        P(("sec", "dev"), None, None),
        P(("sec", "dev"), None, None),
        P(("sec", "dev")),
        P(("sec", "dev"), None),
        P(),
        P("dev", None, None),
        P("dev", None),
        P(None, "dev"),
        P(None, "dev"),
        P("dev", None),
        P(("sec", "dev"), None),
        P(("sec", "dev"), None),
    )
    return jax.shard_map(
        body, mesh=mesh, in_specs=placed, out_specs=P(("sec", "dev"), None), check_vma=False
    )
```

```python
import functools

import jax
import jax.numpy as jnp
from jax import lax
from jax.experimental import pallas as pl
from jax.experimental.pallas import tpu as pltpu
from jax.sharding import PartitionSpec as P

EXPERTS = 4
TOPK = 2
ROWS = 8
GROUP = 32
DIMS = 5
TILE = 256
LANES = 128
TABLE = (
    ((0, 1, 2, 3, 4), 0, 6),
    ((1, 2, 3, 4, 0), 1, 6),
    ((2, 3, 4, 0, 1), 2, 6),
    ((3, 4, 0, 1, 2), 3, 6),
    ((4, 0, 1, 2, 3), 0, 6),
    ((0, 1, 2, 3, 4), 2, 6),
    ((1, 2, 3, 4, 0), 3, 5),
    ((2, 3, 4, 0, 1), 0, 5),
    ((3, 4, 0, 1, 2), 1, 5),
    ((4, 0, 1, 2, 3), 1, 5),
)
LAG = 0
CHUNKS = len(TABLE)
SPREAD = 4
SLOTS = 2 * SPREAD + 3
MASKS = (1, 2, 6, 8, 24)
MESH = pl.DeviceIdType.MESH


def mask_of(code):
    mask = 0
    for dim in range(DIMS):
        if (code >> dim) & 1:
            mask ^= MASKS[dim]
    return mask


def flipped(bits, mask):
    total = 0
    for i, bit in enumerate(bits):
        total = total + (1 << i) * ((1 - bit) if (mask >> i) & 1 else bit)
    return total


class Plan:
    def __init__(self, core):
        self.core = core
        self.blocks = GROUP if core == 0 else GROUP // 2
        self.halvings = 3 if core == 0 else 2
        self.rows = self.blocks * ROWS

    def order(self, chunk):
        if self.core == 0:
            return TABLE[chunk][0]
        return [1 + (TABLE[chunk][1] + i) % 4 for i in range(4)]

    def codes(self):
        return [(code if self.core == 0 else 2 * code) for code in range(self.blocks)]

    def place(self, chunk, code):
        order = self.order(chunk)
        place = 0
        for step, dim in enumerate(order):
            place += ((code >> dim) & 1) << (len(order) - 1 - step)
        return place

    def code(self, chunk, place):
        order = self.order(chunk)
        code = 0
        for step, dim in enumerate(order):
            code += ((place >> (len(order) - 1 - step)) & 1) << dim
        return code


def places():
    section = lax.axis_index("sec")
    me = lax.axis_index("dev")
    bits = [(me // (1 << i)) % 2 for i in range(DIMS)]
    devices = {code: flipped(bits, mask_of(code)) for code in range(GROUP)}
    return section, me, devices


def partner(plan, section, devices, code):
    across = lax.rem(section + 2, 4)
    return (across if plan.core == 1 and code % 2 else section, devices[code])


def greet(plan):
    section, _, devices = places()
    barrier = pltpu.get_barrier_semaphore()
    for code in range(1, GROUP):
        pl.semaphore_signal(
            barrier,
            inc=1,
            device_id=partner(plan, section, devices, code),
            device_id_type=MESH,
        )


def attend(query_ref, length_ref, cache_hbm, cache, by_head, latent_ref, cache_sem, start_loads):
    tokens, heads, _ = query_ref.shape
    latent_width = LANES * len(by_head)
    value_width = LANES
    score_scale = (value_width + query_ref.shape[2] - latent_width) ** (-0.5)
    fetches = []
    for token in range(tokens):
        fetch = pltpu.make_async_copy(cache_hbm.at[token], cache.at[token], cache_sem.at[token])
        fetch.start()
        fetches.append(fetch)
    position = lax.broadcasted_iota(jnp.int32, (heads, cache.shape[2]), 1)
    for token in range(tokens):
        fetches[token].wait()
        if token == 2:
            start_loads()
        scores = jnp.dot(query_ref[token], cache[token], preferred_element_type=jnp.float32)
        usable = position < length_ref[token]
        masked = jnp.where(usable, scores * score_scale, -1e30)
        highest = jnp.max(masked, axis=1, keepdims=True)
        expos = jnp.where(usable, jnp.exp(masked - highest), 0.0)
        weights = expos * (1.0 / jnp.sum(expos, axis=1, keepdims=True))
        mixed = lax.dot_general(
            weights.astype(jnp.bfloat16),
            cache[token, 0:latent_width, :],
            (((1,), (1,)), ((), ())),
            preferred_element_type=jnp.float32,
        )
        for part, lines in enumerate(by_head):
            columns = slice(part * LANES, (part + 1) * LANES)
            lines[pl.ds(token, heads, stride=tokens), :] = mixed[:, columns]
    dests, rows, _ = latent_ref.shape
    for part, lines in enumerate(by_head):
        columns = slice(part * LANES, (part + 1) * LANES)
        latent_ref[:, :, columns] = lines[...].reshape(dests, rows, LANES).astype(jnp.bfloat16)


def work(plan, widths, refs, buffers, loads):
    (
        latent_ref,
        residual_ref,
        gain_ref,
        share_ref,
        value_ref,
        out_ref,
        out_weight,
        gate,
        up,
        down,
        latents,
        left,
        stream,
        square,
        gate_sum,
        up_sum,
        act,
        pass_send,
        pass_recv,
        send_sem,
        recv_sem,
    ) = refs
    partial = buffers[:CHUNKS]
    landings = (buffers[CHUNKS : 2 * CHUNKS], None, buffers[2 * CHUNKS : 3 * CHUNKS])
    rows_of = buffers[3 * CHUNKS :]
    starts = [sum(widths[:k]) for k in range(CHUNKS)]
    section, me, devices = places()
    blocks, rows, halvings = plan.blocks, plan.rows, plan.halvings
    base = pl.ds(0, rows)
    owning = section < 3

    def peer(code):
        return partner(plan, section, devices, code)

    def when_owning(owns, run):
        if plan.core == 0:
            if owns:
                run()
        else:
            pl.when(owning if owns else jnp.logical_not(owning))(run)

    pl.semaphore_wait(pltpu.get_barrier_semaphore(), GROUP - 1)

    def passing(code):
        slot = code if plan.core == 0 else code // 2
        return pltpu.make_async_remote_copy(
            src_ref=latent_ref.at[devices[code]],
            dst_ref=latents.at[slot],
            send_sem=pass_send.at[code],
            recv_sem=pass_recv.at[slot],
            device_id=peer(code),
            device_id_type=MESH,
        )

    def pass_out():
        for code in range(1, GROUP):
            passing(code).start()
        latents[0] = latent_ref[me]

    def pass_in(codes):
        for code in codes:
            passing(code).wait_recv()

    when_owning(True, pass_out)
    if plan.core == 0:
        pass_in(range(1, GROUP))
    else:
        when_owning(True, lambda: pass_in(range(2, GROUP, 2)))
        when_owning(False, lambda: pass_in(range(1, GROUP, 2)))
    for head in range(2):
        lines = latents[pl.ds(0, blocks), head * ROWS : (head + 1) * ROWS, :].astype(jnp.float32)
        lines = lines.reshape(rows, lines.shape[2]).astype(jnp.bfloat16)
        valued = jnp.dot(lines, value_ref[head], preferred_element_type=jnp.float32)
        left[base, head * LANES : (head + 1) * LANES] = valued.astype(jnp.bfloat16)

    started = []

    def copy_of(source, target, phase, chunk, slot, out_slot, code):
        return pltpu.make_async_remote_copy(
            src_ref=source,
            dst_ref=target,
            send_sem=send_sem.at[phase, chunk, out_slot],
            recv_sem=recv_sem.at[phase, chunk, slot],
            device_id=peer(code),
            device_id_type=MESH,
        )

    def go(copy):
        copy.start()
        started.append(copy)
        return copy

    def halving(phase, chunk, step):
        half = (blocks // 2) >> step
        places = pl.ds(half, half)
        slot = 2 * SPREAD + step
        return copy_of(
            partial[chunk].at[places],
            landings[phase][chunk].at[places],
            phase,
            chunk,
            slot,
            slot,
            1 << plan.order(chunk)[step],
        )

    def direct(phase, chunk, place):
        return copy_of(
            partial[chunk].at[place],
            landings[phase][chunk].at[place],
            phase,
            chunk,
            place,
            place,
            plan.code(chunk, place),
        )

    def direct_across(phase, chunk, place):
        return copy_of(
            partial[chunk].at[place],
            landings[phase][chunk].at[16 + place],
            phase,
            chunk,
            SPREAD + place,
            SPREAD + place,
            plan.code(chunk, place) + 1,
        )

    def sum_send(phase, chunk, step):
        if step < halvings:
            go(halving(phase, chunk, step))
            return

        def to_owners():
            for place in range(1, SPREAD):
                direct(phase, chunk, place).start()

        def to_owners_across():
            for place in range(SPREAD):
                direct_across(phase, chunk, place).start()

        when_owning(True, to_owners)
        when_owning(False, to_owners_across)

    def sum_sent(phase):
        def to_owners():
            for chunk in range(CHUNKS):
                for place in range(1, SPREAD):
                    direct(phase, chunk, place).wait_send()

        def to_owners_across():
            for chunk in range(CHUNKS):
                for place in range(SPREAD):
                    direct_across(phase, chunk, place).wait_send()

        when_owning(True, to_owners)
        when_owning(False, to_owners_across)

    def all_sent():
        for copy in started:
            copy.wait_send()
        del started[:]

    def add_rows(phase, chunk, half, first, count):
        @pl.loop(0, count)
        def _(i):
            row = first + i
            partial[chunk][row] = partial[chunk][row] + landings[phase][chunk][half + row]

    def sum_step(phase, chunk, step):
        half = (blocks // 2) >> step
        halving(phase, chunk, step).wait_recv()
        ahead = half // 2 if step < halvings - 1 else 0
        add_rows(phase, chunk, half, ahead, half - ahead)
        sum_send(phase, chunk, step + 1)
        if ahead:
            add_rows(phase, chunk, half, 0, ahead)

    def sum_last(phase, chunk):
        total = partial[chunk][0].astype(jnp.float32)
        for place in range(1, SPREAD):
            direct(phase, chunk, place).wait_recv()
            total = total + landings[phase][chunk][place].astype(jnp.float32)
        if plan.core == 1:
            for place in range(SPREAD):
                direct_across(phase, chunk, place).wait_recv()
                total = total + landings[phase][chunk][16 + place].astype(jnp.float32)
        return total

    def tiled(chunk, one):
        whole = widths[chunk] // TILE

        @pl.loop(0, whole)
        def _(i):
            one(pl.multiple_of(i * TILE, TILE), TILE)

        if widths[chunk] % TILE:
            one(whole * TILE, widths[chunk] % TILE)

    def project(chunk, operand, weight, scale):
        def one(offset, size):
            inner = pl.ds(offset, size)
            outer = pl.ds(pl.multiple_of(starts[chunk] + offset, LANES), size)
            product = jnp.dot(
                operand[base, :], weight[:, outer], preferred_element_type=jnp.float32
            )
            if scale is not None:
                product = product * scale
            for i, code in enumerate(plan.codes()):
                block = product[i * ROWS : (i + 1) * ROWS]
                partial[chunk][plan.place(chunk, code), :, inner] = block.astype(jnp.bfloat16)

        tiled(chunk, one)

    def gather_near(chunk, place):
        return copy_of(
            rows_of[chunk].at[0],
            rows_of[chunk].at[place],
            1,
            chunk,
            place,
            place,
            plan.code(chunk, place),
        )

    def gather_across(chunk, place):
        return copy_of(
            rows_of[chunk].at[0],
            rows_of[chunk].at[place],
            1,
            chunk,
            place,
            SPREAD + place,
            plan.code(chunk, place) + 1,
        )

    def doubling(chunk, step):
        count = (blocks // 2) >> step
        slot = 2 * SPREAD + step
        return copy_of(
            rows_of[chunk].at[pl.ds(0, count)],
            rows_of[chunk].at[pl.ds(count, count)],
            1,
            chunk,
            slot,
            slot,
            1 << plan.order(chunk)[step],
        )

    def attended_rows(chunk):
        columns = pl.ds(starts[chunk], widths[chunk])
        total = residual_ref[:, columns].astype(jnp.float32) + sum_last(0, chunk)
        total = total.astype(jnp.bfloat16)
        stream[:, columns] = total
        total = total.astype(jnp.float32)
        squares = total * total
        folded = sum(squares[:, i : i + LANES] for i in range(0, widths[chunk], LANES))
        square[...] = folded if chunk == 0 else square[...] + folded
        scaled = total * gain_ref[:, columns]
        rows_of[chunk][0, :, : widths[chunk]] = scaled.astype(jnp.bfloat16)
        if chunk == CHUNKS - 1:
            mean = jnp.sum(square[...], axis=1, keepdims=True) / stream.shape[1]
            level = lax.rsqrt(mean + 1e-06)
            coarse = level.astype(jnp.bfloat16).astype(jnp.float32)
            lane = lax.broadcasted_iota(jnp.int32, (ROWS, LANES), 1)
            extra = share_ref[...].astype(jnp.float32)
            extra = jnp.where(lane == 2 * EXPERTS, coarse, extra)
            extra = jnp.where(lane == 2 * EXPERTS + 1, level - coarse, extra)
            rows_of[chunk][0, :, widths[chunk] :] = extra.astype(jnp.bfloat16)
        for place in range(SPREAD):
            if place:
                gather_near(chunk, place).start()
            if plan.core == 1:
                gather_across(chunk, place).start()

    def first_doubling(chunk):
        when_owning(False, lambda: gather_across(chunk, 0).wait_recv())
        for place in range(1, SPREAD):
            gather_near(chunk, place).wait_recv()
        go(doubling(chunk, halvings - 1))

    def stacked(chunk, columns):
        lines = [
            rows_of[chunk][plan.place(chunk, code), :, columns].astype(jnp.float32)
            for code in plan.codes()
        ]
        return jnp.concatenate(lines, axis=0)

    def hidden_sums(chunk):
        doubling(chunk, 0).wait_recv()

        def one(offset, size):
            outer = pl.ds(pl.multiple_of(starts[chunk] + offset, LANES), size)
            lines = stacked(chunk, pl.ds(offset, size)).astype(jnp.bfloat16)
            gate_sum[base, :] += jnp.dot(lines, gate[outer, :], preferred_element_type=jnp.float32)
            up_sum[base, :] += jnp.dot(lines, up[outer, :], preferred_element_type=jnp.float32)

        tiled(chunk, one)

    def staggered(count, stage):
        for time in range(count + LAG * (CHUNKS // DIMS - 1)):
            for group in range(CHUNKS // DIMS):
                if 0 <= time - LAG * group < count:
                    for chunk in range(group * DIMS, (group + 1) * DIMS):
                        stage(chunk, time - LAG * group)

    def until_hidden(chunk, step):
        if step == 0:
            project(chunk, left, out_weight, None)
            sum_send(0, chunk, 0)
        elif step <= halvings:
            sum_step(0, chunk, step - 1)
        elif step == halvings + 1:
            when_owning(True, functools.partial(attended_rows, chunk))
        elif step == halvings + 2:
            first_doubling(chunk)
        elif step <= 2 * halvings + 1:
            done = step - halvings - 2
            doubling(chunk, halvings - done).wait_recv()
            go(doubling(chunk, halvings - done - 1))
        else:
            hidden_sums(chunk)

    def until_output(chunk, step):
        if step == 0:
            project(chunk, act, down, share)
            sum_send(2, chunk, 0)
        elif step <= halvings:
            sum_step(2, chunk, step - 1)
        else:
            when_owning(True, functools.partial(result_rows, chunk))

    def result_rows(chunk):
        columns = pl.ds(starts[chunk], widths[chunk])
        result = stream[:, columns].astype(jnp.float32) + sum_last(2, chunk)
        out_ref[:, columns] = result.astype(jnp.bfloat16)

    gate_sum[base, :] = jnp.zeros((rows, gate_sum.shape[1]), jnp.float32)
    up_sum[base, :] = jnp.zeros((rows, up_sum.shape[1]), jnp.float32)
    for load in loads[:3]:
        load.wait()
    staggered(2 * halvings + 3, until_hidden)
    shares = stacked(CHUNKS - 1, pl.ds(widths[CHUNKS - 1], LANES))
    lane = lax.broadcasted_iota(jnp.int32, shares.shape, 1)
    expert = me // (GROUP // EXPERTS)

    def picked(first, second):
        chosen = (lane == first) | (lane == second)
        return jnp.sum(jnp.where(chosen, shares, 0.0), axis=1, keepdims=True)

    share = picked(expert, expert + EXPERTS)
    level = picked(2 * EXPERTS, 2 * EXPERTS + 1)
    hidden = gate_sum[base, :] * level
    hidden = hidden / (1.0 + jnp.exp(-hidden)) * (up_sum[base, :] * level)
    act[base, :] = hidden.astype(jnp.bfloat16)
    loads[3].wait()
    all_sent()
    sum_sent(0)
    staggered(halvings + 2, until_output)

    def finish():
        for code in range(1, GROUP):
            passing(code).wait_send()
        for chunk in range(CHUNKS):
            for place in range(SPREAD):
                if place:
                    gather_near(chunk, place).wait_send()
                if plan.core == 1:
                    gather_across(chunk, place).wait_send()

    def blank():
        out_ref[...] = jnp.zeros_like(out_ref)

    when_owning(True, finish)
    when_owning(False, blank)
    all_sent()
    sum_sent(2)


def layer_kernel(
    widths,
    length_ref,
    query_ref,
    residual_ref,
    gain_ref,
    share_ref,
    value_ref,
    cache_hbm,
    out_weight_hbm,
    gate_hbm,
    up_hbm,
    down_hbm,
    out_ref,
    out_weight,
    gate,
    up,
    down,
    cache,
    latent_ref,
    latents,
    left,
    stream,
    square,
    gate_sum,
    up_sum,
    act,
    cache_sem,
    load_sem,
    pass_send,
    pass_recv,
    send_sem,
    recv_sem,
    *buffers,
):
    parts = latent_ref.shape[2] // LANES
    by_head, buffers = buffers[:parts], buffers[parts:]
    loads = [
        pltpu.make_async_copy(source, target, load_sem.at[i])
        for i, (source, target) in enumerate(
            ((out_weight_hbm, out_weight), (gate_hbm, gate), (up_hbm, up), (down_hbm, down))
        )
    ]
    refs = (latent_ref, residual_ref, gain_ref, share_ref, value_ref, out_ref)
    refs += (out_weight, gate, up, down, latents, left, stream, square, gate_sum, up_sum, act)
    refs += (pass_send, pass_recv, send_sem, recv_sem)
    section = lax.axis_index("sec")
    core = section % 2
    for number in range(2):
        pl.when(core == number)(functools.partial(greet, Plan(number)))

    def start_loads():
        for load in loads:
            load.start()

    pl.when(section < 3)(
        lambda: attend(
            query_ref, length_ref, cache_hbm, cache, by_head, latent_ref, cache_sem, start_loads
        )
    )
    pl.when(section == 3)(start_loads)
    for number in range(2):
        pl.when(core == number)(
            functools.partial(work, Plan(number), widths, refs, buffers, loads)
        )


def layer(lengths, queries, residual, gain, shares, value_up, cache, *weights):
    width = residual.shape[1]
    widths = [LANES * units for _, _, units in TABLE]
    hidden = weights[1].shape[1]
    tokens, heads, _ = queries.shape
    latent_width = value_up.shape[1]
    bf16, f32 = jnp.bfloat16, jnp.float32
    vmem = pl.BlockSpec(memory_space=pltpu.VMEM)
    hbm = pl.BlockSpec(memory_space=pl.ANY)
    latents = pltpu.VMEM((GROUP, heads * tokens // GROUP, latent_width), bf16)
    scratch = [pltpu.VMEM(weight.shape, bf16) for weight in weights]
    scratch += [
        pltpu.VMEM(cache.shape, bf16),
        latents,
        latents,
        pltpu.VMEM((GROUP * ROWS, 2 * LANES), bf16),
        pltpu.VMEM((ROWS, width), bf16),
        pltpu.VMEM((ROWS, LANES), f32),
        pltpu.VMEM((GROUP * ROWS, hidden), f32),
        pltpu.VMEM((GROUP * ROWS, hidden), f32),
        pltpu.VMEM((GROUP * ROWS, hidden), bf16),
        pltpu.SemaphoreType.DMA((tokens,)),
        pltpu.SemaphoreType.DMA((4,)),
        pltpu.SemaphoreType.DMA((GROUP,)),
        pltpu.SemaphoreType.DMA((GROUP,)),
        pltpu.SemaphoreType.DMA((3, CHUNKS, SLOTS)),
        pltpu.SemaphoreType.DMA((3, CHUNKS, SLOTS)),
    ]
    scratch += [pltpu.VMEM((heads * tokens, LANES), f32)] * (latent_width // LANES)
    scratch += [pltpu.VMEM((GROUP, ROWS, w), bf16) for w in widths] * 3
    extra = [0] * (CHUNKS - 1) + [LANES]
    scratch += [pltpu.VMEM((GROUP, ROWS, w + e), bf16) for w, e in zip(widths, extra)]
    return pl.pallas_call(
        functools.partial(layer_kernel, widths),
        out_shape=jax.ShapeDtypeStruct(residual.shape, bf16),
        in_specs=[pl.BlockSpec(memory_space=pltpu.SMEM)] + [vmem] * 5 + [hbm] * 5,
        out_specs=vmem,
        scratch_shapes=scratch,
        compiler_params=pltpu.CompilerParams(
            collective_id=0, has_side_effects=True, vmem_limit_bytes=58 * 1024 * 1024
        ),
    )(lengths, queries, residual, gain, shares, value_up, cache, *weights)


def body(
    queries,
    latent_cache,
    cache_length,
    residual,
    norm_gain,
    value_up,
    out_weight,
    gate_weight,
    up_weight,
    down_weight,
    expert_index,
    gate_level,
):
    levels = gate_level.astype(jnp.float32)
    mix = levels / jnp.sum(levels, axis=1, keepdims=True)
    named = expert_index[:, :, None] == jnp.arange(EXPERTS, dtype=jnp.int32)[None, None, :]
    share = jnp.sum(jnp.where(named, mix[:, :, None], 0.0), axis=1)
    coarse = share.astype(jnp.bfloat16)
    fine = (share - coarse.astype(jnp.float32)).astype(jnp.bfloat16)
    shares = jnp.pad(jnp.concatenate([coarse, fine], axis=1), ((0, 0), (0, 128 - 2 * EXPERTS)))
    return layer(
        cache_length,
        queries,
        residual,
        norm_gain.reshape(1, -1),
        shares,
        value_up,
        jnp.swapaxes(latent_cache, 1, 2),
        out_weight,
        gate_weight,
        up_weight,
        down_weight,
    )


def solution(mesh):
    placed = (
        P(("sec", "dev"), None, None),
        P(("sec", "dev"), None, None),
        P(("sec", "dev")),
        P(("sec", "dev"), None),
        P(),
        P("dev", None, None),
        P("dev", None),
        P(None, "dev"),
        P(None, "dev"),
        P("dev", None),
        P(("sec", "dev"), None),
        P(("sec", "dev"), None),
    )
    return jax.shard_map(
        body, mesh=mesh, in_specs=placed, out_specs=P(("sec", "dev"), None), check_vma=False
    )
```

```python
import functools

import jax
import jax.numpy as jnp
from jax import lax
from jax.experimental import pallas as pl
from jax.experimental.pallas import tpu as pltpu
from jax.sharding import PartitionSpec as P

EXPERTS = 4
TOPK = 2
ROWS = 8
GROUP = 32
DIMS = 5
TILE = 256
LANES = 128
TABLE = (
    ((0, 1, 2, 3, 4), 0, 6),
    ((1, 2, 3, 4, 0), 1, 6),
    ((2, 3, 4, 0, 1), 2, 6),
    ((3, 4, 0, 1, 2), 3, 6),
    ((4, 0, 1, 2, 3), 0, 6),
    ((0, 1, 2, 3, 4), 2, 6),
    ((1, 2, 3, 4, 0), 3, 5),
    ((2, 3, 4, 0, 1), 0, 5),
    ((3, 4, 0, 1, 2), 1, 5),
    ((4, 0, 1, 2, 3), 1, 5),
)
LAG = 0
CHUNKS = len(TABLE)
SPREAD = 4
NEAR, FAR, HALVED = 0, 1, 2
SLOTS = HALVED + 3
MASKS = (1, 2, 6, 8, 24)
MESH = pl.DeviceIdType.MESH


def mask_of(code):
    mask = 0
    for dim in range(DIMS):
        if (code >> dim) & 1:
            mask ^= MASKS[dim]
    return mask


def flipped(bits, mask):
    total = 0
    for i, bit in enumerate(bits):
        total = total + (1 << i) * ((1 - bit) if (mask >> i) & 1 else bit)
    return total


class Plan:
    def __init__(self, core):
        self.core = core
        self.blocks = GROUP if core == 0 else GROUP // 2
        self.halvings = 3 if core == 0 else 2
        self.rows = self.blocks * ROWS

    def order(self, chunk):
        if self.core == 0:
            return TABLE[chunk][0]
        return [1 + (TABLE[chunk][1] + i) % 4 for i in range(4)]

    def codes(self):
        return [(code if self.core == 0 else 2 * code) for code in range(self.blocks)]

    def place(self, chunk, code):
        order = self.order(chunk)
        place = 0
        for step, dim in enumerate(order):
            place += ((code >> dim) & 1) << (len(order) - 1 - step)
        return place

    def code(self, chunk, place):
        order = self.order(chunk)
        code = 0
        for step, dim in enumerate(order):
            code += ((place >> (len(order) - 1 - step)) & 1) << dim
        return code


def places():
    section = lax.axis_index("sec")
    me = lax.axis_index("dev")
    bits = [(me // (1 << i)) % 2 for i in range(DIMS)]
    devices = {code: flipped(bits, mask_of(code)) for code in range(GROUP)}
    return section, me, devices


def partner(plan, section, devices, code):
    across = lax.rem(section + 2, 4)
    return (across if plan.core == 1 and code % 2 else section, devices[code])


def greet(plan):
    section, _, devices = places()
    barrier = pltpu.get_barrier_semaphore()
    for code in range(1, GROUP):
        pl.semaphore_signal(
            barrier,
            inc=1,
            device_id=partner(plan, section, devices, code),
            device_id_type=MESH,
        )


def attend(query_ref, length_ref, cache_hbm, cache, by_head, latent_ref, cache_sem, start_loads):
    tokens, heads, _ = query_ref.shape
    latent_width = LANES * len(by_head)
    value_width = LANES
    score_scale = (value_width + query_ref.shape[2] - latent_width) ** (-0.5)
    fetches = []
    for token in range(tokens):
        fetch = pltpu.make_async_copy(cache_hbm.at[token], cache.at[token], cache_sem.at[token])
        fetch.start()
        fetches.append(fetch)
    position = lax.broadcasted_iota(jnp.int32, (heads, cache.shape[2]), 1)
    for token in range(tokens):
        fetches[token].wait()
        if token == 2:
            start_loads()
        scores = jnp.dot(query_ref[token], cache[token], preferred_element_type=jnp.float32)
        usable = position < length_ref[token]
        masked = jnp.where(usable, scores * score_scale, -1e30)
        highest = jnp.max(masked, axis=1, keepdims=True)
        expos = jnp.where(usable, jnp.exp(masked - highest), 0.0)
        weights = expos * (1.0 / jnp.sum(expos, axis=1, keepdims=True))
        mixed = lax.dot_general(
            weights.astype(jnp.bfloat16),
            cache[token, 0:latent_width, :],
            (((1,), (1,)), ((), ())),
            preferred_element_type=jnp.float32,
        )
        for part, lines in enumerate(by_head):
            columns = slice(part * LANES, (part + 1) * LANES)
            lines[pl.ds(token, heads, stride=tokens), :] = mixed[:, columns]
    dests, rows, _ = latent_ref.shape
    for part, lines in enumerate(by_head):
        columns = slice(part * LANES, (part + 1) * LANES)
        latent_ref[:, :, columns] = lines[...].reshape(dests, rows, LANES).astype(jnp.bfloat16)


def work(plan, widths, refs, buffers, loads):
    (
        latent_ref,
        residual_ref,
        gain_ref,
        expert_ref,
        level_ref,
        value_ref,
        out_ref,
        out_weight,
        gate,
        up,
        down,
        latents,
        left,
        stream,
        square,
        gate_sum,
        up_sum,
        act,
        pass_send,
        pass_recv,
        send_sem,
        recv_sem,
    ) = refs
    partial = buffers[:CHUNKS]
    landings = (buffers[CHUNKS : 2 * CHUNKS], None, buffers[2 * CHUNKS : 3 * CHUNKS])
    rows_of = buffers[3 * CHUNKS :]
    starts = [sum(widths[:k]) for k in range(CHUNKS)]
    section, me, devices = places()
    blocks, rows, halvings = plan.blocks, plan.rows, plan.halvings
    base = pl.ds(0, rows)
    owning = section < 3

    def peer(code):
        return partner(plan, section, devices, code)

    def when_owning(owns, run):
        if plan.core == 0:
            if owns:
                run()
        else:
            pl.when(owning if owns else jnp.logical_not(owning))(run)

    pl.semaphore_wait(pltpu.get_barrier_semaphore(), GROUP - 1)

    def passing(code):
        slot = code if plan.core == 0 else code // 2
        return pltpu.make_async_remote_copy(
            src_ref=latent_ref.at[devices[code]],
            dst_ref=latents.at[slot],
            send_sem=pass_send,
            recv_sem=pass_recv,
            device_id=peer(code),
            device_id_type=MESH,
        )

    def passed(slots):
        return pltpu.make_async_remote_copy(
            src_ref=latent_ref.at[slots],
            dst_ref=latents.at[slots],
            send_sem=pass_send,
            recv_sem=pass_recv,
            device_id=peer(1),
            device_id_type=MESH,
        )

    def pass_out():
        for code in range(1, GROUP):
            passing(code).start()
        latents[0] = latent_ref[me]
        passed(pl.ds(1, blocks - 1)).wait_recv()

    when_owning(True, pass_out)
    when_owning(False, lambda: passed(pl.ds(0, blocks)).wait_recv())
    for head in range(2):
        lines = latents[pl.ds(0, blocks), head * ROWS : (head + 1) * ROWS, :].astype(jnp.float32)
        lines = lines.reshape(rows, lines.shape[2]).astype(jnp.bfloat16)
        valued = jnp.dot(lines, value_ref[head], preferred_element_type=jnp.float32)
        left[base, head * LANES : (head + 1) * LANES] = valued.astype(jnp.bfloat16)

    def copy_of(source, target, phase, chunk, slot, code):
        return pltpu.make_async_remote_copy(
            src_ref=source,
            dst_ref=target,
            send_sem=send_sem.at[phase % 2, chunk],
            recv_sem=recv_sem.at[phase % 2, chunk, slot],
            device_id=peer(code),
            device_id_type=MESH,
        )

    def arrived(buffer, places, phase, chunk, slot):
        lines = buffer[chunk].at[places]
        copy_of(lines, lines, phase, chunk, slot, 1).wait_recv()

    def sent(buffer, phase, count):
        for chunk in range(CHUNKS):
            lines = buffer[chunk].at[pl.ds(0, count)]
            copy_of(lines, lines, phase, chunk, NEAR, 1).wait_send()

    def halving(phase, chunk, step):
        half = (blocks // 2) >> step
        places = pl.ds(half, half)
        return copy_of(
            partial[chunk].at[places],
            landings[phase][chunk].at[places],
            phase,
            chunk,
            HALVED + step,
            1 << plan.order(chunk)[step],
        )

    def sum_send(phase, chunk, step):
        if step < halvings:
            halving(phase, chunk, step).start()
            return

        def to_owners():
            for place in range(1, SPREAD):
                copy_of(
                    partial[chunk].at[place],
                    landings[phase][chunk].at[place],
                    phase,
                    chunk,
                    NEAR,
                    plan.code(chunk, place),
                ).start()

        def to_owners_across():
            for place in range(SPREAD):
                copy_of(
                    partial[chunk].at[place],
                    landings[phase][chunk].at[16 + place],
                    phase,
                    chunk,
                    FAR,
                    plan.code(chunk, place) + 1,
                ).start()

        when_owning(True, to_owners)
        when_owning(False, to_owners_across)

    def sum_sent(phase):
        when_owning(True, lambda: sent(partial, phase, blocks - 1))
        when_owning(False, lambda: sent(partial, phase, blocks))

    def add_rows(phase, chunk, half, first, count):
        @pl.loop(0, count)
        def _(i):
            row = first + i
            partial[chunk][row] = partial[chunk][row] + landings[phase][chunk][half + row]

    def sum_step(phase, chunk, step):
        half = (blocks // 2) >> step
        halving(phase, chunk, step).wait_recv()
        ahead = half // 2 if step < halvings - 1 else 0
        add_rows(phase, chunk, half, ahead, half - ahead)
        sum_send(phase, chunk, step + 1)
        if ahead:
            add_rows(phase, chunk, half, 0, ahead)

    def sum_last(phase, chunk):
        total = partial[chunk][0].astype(jnp.float32)
        arrived(landings[phase], pl.ds(1, SPREAD - 1), phase, chunk, NEAR)
        for place in range(1, SPREAD):
            total = total + landings[phase][chunk][place].astype(jnp.float32)
        if plan.core == 1:
            arrived(landings[phase], pl.ds(16, SPREAD), phase, chunk, FAR)
            for place in range(SPREAD):
                total = total + landings[phase][chunk][16 + place].astype(jnp.float32)
        return total

    def tiled(chunk, one):
        whole = widths[chunk] // TILE

        @pl.loop(0, whole)
        def _(i):
            one(pl.multiple_of(i * TILE, TILE), TILE)

        if widths[chunk] % TILE:
            one(whole * TILE, widths[chunk] % TILE)

    def project(chunk, operand, weight, scale):
        def one(offset, size):
            inner = pl.ds(offset, size)
            outer = pl.ds(pl.multiple_of(starts[chunk] + offset, LANES), size)
            product = jnp.dot(
                operand[base, :], weight[:, outer], preferred_element_type=jnp.float32
            )
            if scale is not None:
                product = product * scale
            for i, code in enumerate(plan.codes()):
                block = product[i * ROWS : (i + 1) * ROWS]
                partial[chunk][plan.place(chunk, code), :, inner] = block.astype(jnp.bfloat16)

        tiled(chunk, one)

    def gather(chunk, place, across):
        return copy_of(
            rows_of[chunk].at[0],
            rows_of[chunk].at[place],
            1,
            chunk,
            NEAR,
            plan.code(chunk, place) + across,
        )

    def doubling(chunk, step):
        count = (blocks // 2) >> step
        return copy_of(
            rows_of[chunk].at[pl.ds(0, count)],
            rows_of[chunk].at[pl.ds(count, count)],
            1,
            chunk,
            HALVED + step,
            1 << plan.order(chunk)[step],
        )

    def share_lanes():
        lane = lax.broadcasted_iota(jnp.int32, (ROWS, LANES), 1)
        own = lax.broadcasted_iota(jnp.int32, (ROWS, ROWS), 0) == lax.broadcasted_iota(
            jnp.int32, (ROWS, ROWS), 1
        )

        def column(ref, k):
            line = jnp.broadcast_to(ref[k : k + 1, :].astype(jnp.float32), (ROWS, ROWS))
            return jnp.sum(jnp.where(own, line, 0.0), axis=1, keepdims=True)

        levels = [column(level_ref, k) for k in range(TOPK)]
        named = jnp.where(lane < EXPERTS, lane, lane - EXPERTS).astype(jnp.float32)
        mixed = jnp.zeros((ROWS, LANES), jnp.float32)
        for k in range(TOPK):
            mixed += jnp.where(named == column(expert_ref, k), levels[k] / sum(levels), 0.0)
        coarse = mixed.astype(jnp.bfloat16).astype(jnp.float32)
        return lane, jnp.where(lane < EXPERTS, coarse, mixed - coarse)

    def attended_rows(chunk):
        columns = pl.ds(starts[chunk], widths[chunk])
        total = residual_ref[:, columns].astype(jnp.float32) + sum_last(0, chunk)
        total = total.astype(jnp.bfloat16)
        stream[:, columns] = total
        total = total.astype(jnp.float32)
        squares = total * total
        folded = sum(squares[:, i : i + LANES] for i in range(0, widths[chunk], LANES))
        square[...] = folded if chunk == 0 else square[...] + folded
        scaled = total * gain_ref[:, columns]
        rows_of[chunk][0, :, : widths[chunk]] = scaled.astype(jnp.bfloat16)
        if chunk == CHUNKS - 1:
            mean = jnp.sum(square[...], axis=1, keepdims=True) / stream.shape[1]
            level = lax.rsqrt(mean + 1e-06)
            coarse = level.astype(jnp.bfloat16).astype(jnp.float32)
            lane, extra = share_lanes()
            extra = jnp.where(lane == 2 * EXPERTS, coarse, extra)
            extra = jnp.where(lane == 2 * EXPERTS + 1, level - coarse, extra)
            rows_of[chunk][0, :, widths[chunk] :] = extra.astype(jnp.bfloat16)
        for place in range(SPREAD):
            if place:
                gather(chunk, place, 0).start()
            if plan.core == 1:
                gather(chunk, place, 1).start()

    def first_doubling(chunk):
        when_owning(True, lambda: arrived(rows_of, pl.ds(1, SPREAD - 1), 1, chunk, NEAR))
        when_owning(False, lambda: arrived(rows_of, pl.ds(0, SPREAD), 1, chunk, NEAR))
        doubling(chunk, halvings - 1).start()

    def stacked(chunk, columns):
        lines = [
            rows_of[chunk][plan.place(chunk, code), :, columns].astype(jnp.float32)
            for code in plan.codes()
        ]
        return jnp.concatenate(lines, axis=0)

    def hidden_sums(chunk):
        doubling(chunk, 0).wait_recv()

        def one(offset, size):
            outer = pl.ds(pl.multiple_of(starts[chunk] + offset, LANES), size)
            lines = stacked(chunk, pl.ds(offset, size)).astype(jnp.bfloat16)
            gate_sum[base, :] += jnp.dot(lines, gate[outer, :], preferred_element_type=jnp.float32)
            up_sum[base, :] += jnp.dot(lines, up[outer, :], preferred_element_type=jnp.float32)

        tiled(chunk, one)

    def staggered(count, stage):
        for time in range(count + LAG * (CHUNKS // DIMS - 1)):
            for group in range(CHUNKS // DIMS):
                if 0 <= time - LAG * group < count:
                    for chunk in range(group * DIMS, (group + 1) * DIMS):
                        stage(chunk, time - LAG * group)

    def until_hidden(chunk, step):
        if step == 0:
            project(chunk, left, out_weight, None)
            sum_send(0, chunk, 0)
        elif step <= halvings:
            sum_step(0, chunk, step - 1)
        elif step == halvings + 1:
            when_owning(True, functools.partial(attended_rows, chunk))
        elif step == halvings + 2:
            first_doubling(chunk)
        elif step <= 2 * halvings + 1:
            done = step - halvings - 2
            doubling(chunk, halvings - done).wait_recv()
            doubling(chunk, halvings - done - 1).start()
        else:
            hidden_sums(chunk)

    def until_output(chunk, step):
        if step == 0:
            project(chunk, act, down, share)
            sum_send(2, chunk, 0)
        elif step <= halvings:
            sum_step(2, chunk, step - 1)
        else:
            when_owning(True, functools.partial(result_rows, chunk))

    def result_rows(chunk):
        columns = pl.ds(starts[chunk], widths[chunk])
        result = stream[:, columns].astype(jnp.float32) + sum_last(2, chunk)
        out_ref[:, columns] = result.astype(jnp.bfloat16)

    gate_sum[base, :] = jnp.zeros((rows, gate_sum.shape[1]), jnp.float32)
    up_sum[base, :] = jnp.zeros((rows, up_sum.shape[1]), jnp.float32)
    for load in loads[:3]:
        load.wait()
    staggered(2 * halvings + 3, until_hidden)
    shares = stacked(CHUNKS - 1, pl.ds(widths[CHUNKS - 1], LANES))
    lane = lax.broadcasted_iota(jnp.int32, shares.shape, 1)
    expert = me // (GROUP // EXPERTS)

    def picked(first, second):
        chosen = (lane == first) | (lane == second)
        return jnp.sum(jnp.where(chosen, shares, 0.0), axis=1, keepdims=True)

    share = picked(expert, expert + EXPERTS)
    level = picked(2 * EXPERTS, 2 * EXPERTS + 1)
    hidden = gate_sum[base, :] * level
    hidden = hidden / (1.0 + jnp.exp(-hidden)) * (up_sum[base, :] * level)
    act[base, :] = hidden.astype(jnp.bfloat16)
    loads[3].wait()
    sum_sent(0)
    staggered(halvings + 2, until_output)

    def finish():
        passed(pl.ds(0, GROUP - 1)).wait_send()
        near = SPREAD - 1 if plan.core == 0 else 2 * SPREAD - 1
        sent(rows_of, 1, blocks - SPREAD + near)

    def blank():
        out_ref[...] = jnp.zeros_like(out_ref)
        sent(rows_of, 1, blocks - SPREAD)

    when_owning(True, finish)
    when_owning(False, blank)
    sum_sent(2)


def layer_kernel(
    widths,
    length_ref,
    query_ref,
    residual_ref,
    gain_ref,
    expert_ref,
    level_ref,
    value_ref,
    cache_hbm,
    out_weight_hbm,
    gate_hbm,
    up_hbm,
    down_hbm,
    out_ref,
    out_weight,
    gate,
    up,
    down,
    cache,
    latent_ref,
    latents,
    left,
    stream,
    square,
    gate_sum,
    up_sum,
    act,
    cache_sem,
    load_sem,
    pass_send,
    pass_recv,
    send_sem,
    recv_sem,
    *buffers,
):
    parts = latent_ref.shape[2] // LANES
    by_head, buffers = buffers[:parts], buffers[parts:]
    loads = [
        pltpu.make_async_copy(source, target, load_sem.at[i])
        for i, (source, target) in enumerate(
            ((out_weight_hbm, out_weight), (gate_hbm, gate), (up_hbm, up), (down_hbm, down))
        )
    ]
    refs = (latent_ref, residual_ref, gain_ref, expert_ref, level_ref, value_ref, out_ref)
    refs += (out_weight, gate, up, down, latents, left, stream, square, gate_sum, up_sum, act)
    refs += (pass_send, pass_recv, send_sem, recv_sem)
    section = lax.axis_index("sec")
    core = section % 2
    for number in range(2):
        pl.when(core == number)(functools.partial(greet, Plan(number)))

    def start_loads():
        for load in loads:
            load.start()

    pl.when(section < 3)(
        lambda: attend(
            query_ref, length_ref, cache_hbm, cache, by_head, latent_ref, cache_sem, start_loads
        )
    )
    pl.when(section == 3)(start_loads)
    for number in range(2):
        pl.when(core == number)(
            functools.partial(work, Plan(number), widths, refs, buffers, loads)
        )


def layer(lengths, queries, residual, gain, experts, levels, value_up, cache, *weights):
    width = residual.shape[1]
    widths = [LANES * units for _, _, units in TABLE]
    hidden = weights[1].shape[1]
    tokens, heads, _ = queries.shape
    latent_width = value_up.shape[1]
    bf16, f32 = jnp.bfloat16, jnp.float32
    vmem = pl.BlockSpec(memory_space=pltpu.VMEM)
    hbm = pl.BlockSpec(memory_space=pl.ANY)
    latents = pltpu.VMEM((GROUP, heads * tokens // GROUP, latent_width), bf16)
    scratch = [pltpu.VMEM(weight.shape, bf16) for weight in weights]
    scratch += [
        pltpu.VMEM(cache.shape, bf16),
        latents,
        latents,
        pltpu.VMEM((GROUP * ROWS, 2 * LANES), bf16),
        pltpu.VMEM((ROWS, width), bf16),
        pltpu.VMEM((ROWS, LANES), f32),
        pltpu.VMEM((GROUP * ROWS, hidden), f32),
        pltpu.VMEM((GROUP * ROWS, hidden), f32),
        pltpu.VMEM((GROUP * ROWS, hidden), bf16),
        pltpu.SemaphoreType.DMA((tokens,)),
        pltpu.SemaphoreType.DMA((4,)),
        pltpu.SemaphoreType.DMA,
        pltpu.SemaphoreType.DMA,
        pltpu.SemaphoreType.DMA((2, CHUNKS)),
        pltpu.SemaphoreType.DMA((2, CHUNKS, SLOTS)),
    ]
    scratch += [pltpu.VMEM((heads * tokens, LANES), f32)] * (latent_width // LANES)
    scratch += [pltpu.VMEM((GROUP, ROWS, w), bf16) for w in widths] * 3
    extra = [0] * (CHUNKS - 1) + [LANES]
    scratch += [pltpu.VMEM((GROUP, ROWS, w + e), bf16) for w, e in zip(widths, extra)]
    return pl.pallas_call(
        functools.partial(layer_kernel, widths),
        out_shape=jax.ShapeDtypeStruct(residual.shape, bf16),
        in_specs=[pl.BlockSpec(memory_space=pltpu.SMEM)] + [vmem] * 6 + [hbm] * 5,
        out_specs=vmem,
        scratch_shapes=scratch,
        compiler_params=pltpu.CompilerParams(
            collective_id=0, has_side_effects=True, vmem_limit_bytes=58 * 1024 * 1024
        ),
    )(lengths, queries, residual, gain, experts, levels, value_up, cache, *weights)


def body(
    queries,
    latent_cache,
    cache_length,
    residual,
    norm_gain,
    value_up,
    out_weight,
    gate_weight,
    up_weight,
    down_weight,
    expert_index,
    gate_level,
):
    return layer(
        cache_length,
        queries,
        residual,
        norm_gain.reshape(1, -1),
        expert_index.T,
        gate_level.T,
        value_up,
        jnp.swapaxes(latent_cache, 1, 2),
        out_weight,
        gate_weight,
        up_weight,
        down_weight,
    )


def solution(mesh):
    placed = (
        P(("sec", "dev"), None, None),
        P(("sec", "dev"), None, None),
        P(("sec", "dev")),
        P(("sec", "dev"), None),
        P(),
        P("dev", None, None),
        P("dev", None),
        P(None, "dev"),
        P(None, "dev"),
        P("dev", None),
        P(("sec", "dev"), None),
        P(("sec", "dev"), None),
    )
    return jax.shard_map(
        body, mesh=mesh, in_specs=placed, out_specs=P(("sec", "dev"), None), check_vma=False
    )
```

```python
import functools

import jax
import jax.numpy as jnp
from jax import lax
from jax.experimental import pallas as pl
from jax.experimental.pallas import tpu as pltpu
from jax.sharding import PartitionSpec as P

EXPERTS = 4
TOPK = 2
ROWS = 8
GROUP = 32
DIMS = 5
TILE = 256
LANES = 128
TABLE = (
    ((0, 1, 2, 3, 4), 0, 3),
    ((1, 2, 3, 4, 0), 1, 3),
    ((2, 3, 4, 0, 1), 2, 3),
    ((3, 4, 0, 1, 2), 3, 3),
    ((4, 0, 1, 2, 3), 0, 3),
    ((0, 1, 2, 3, 4), 1, 3),
    ((1, 2, 3, 4, 0), 2, 3),
    ((2, 3, 4, 0, 1), 3, 3),
    ((3, 4, 0, 1, 2), 0, 3),
    ((4, 0, 1, 2, 3), 1, 3),
    ((0, 1, 2, 3, 4), 2, 3),
    ((1, 2, 3, 4, 0), 3, 3),
    ((2, 3, 4, 0, 1), 0, 3),
    ((3, 4, 0, 1, 2), 1, 3),
    ((4, 0, 1, 2, 3), 2, 3),
    ((0, 1, 2, 3, 4), 3, 3),
    ((1, 2, 3, 4, 0), 0, 2),
    ((2, 3, 4, 0, 1), 1, 2),
    ((3, 4, 0, 1, 2), 2, 2),
    ((4, 0, 1, 2, 3), 3, 2),
)
LAG = 0
CHUNKS = len(TABLE)
SPREAD = 4
NEAR, FAR, HALVED = 0, 1, 2
SLOTS = HALVED + 3
MASKS = (1, 2, 6, 8, 24)
MESH = pl.DeviceIdType.MESH


def mask_of(code):
    mask = 0
    for dim in range(DIMS):
        if (code >> dim) & 1:
            mask ^= MASKS[dim]
    return mask


def flipped(bits, mask):
    total = 0
    for i, bit in enumerate(bits):
        total = total + (1 << i) * ((1 - bit) if (mask >> i) & 1 else bit)
    return total


class Plan:
    def __init__(self, core):
        self.core = core
        self.blocks = GROUP if core == 0 else GROUP // 2
        self.halvings = 3 if core == 0 else 2
        self.rows = self.blocks * ROWS

    def order(self, chunk):
        if self.core == 0:
            return TABLE[chunk][0]
        return [1 + (TABLE[chunk][1] + i) % 4 for i in range(4)]

    def codes(self):
        return [(code if self.core == 0 else 2 * code) for code in range(self.blocks)]

    def place(self, chunk, code):
        order = self.order(chunk)
        place = 0
        for step, dim in enumerate(order):
            place += ((code >> dim) & 1) << (len(order) - 1 - step)
        return place

    def code(self, chunk, place):
        order = self.order(chunk)
        code = 0
        for step, dim in enumerate(order):
            code += ((place >> (len(order) - 1 - step)) & 1) << dim
        return code


def places():
    section = lax.axis_index("sec")
    me = lax.axis_index("dev")
    bits = [(me // (1 << i)) % 2 for i in range(DIMS)]
    devices = {code: flipped(bits, mask_of(code)) for code in range(GROUP)}
    return section, me, devices


def partner(plan, section, devices, code):
    across = lax.rem(section + 2, 4)
    return (across if plan.core == 1 and code % 2 else section, devices[code])


def greet(plan):
    section, _, devices = places()
    barrier = pltpu.get_barrier_semaphore()
    for code in range(1, GROUP):
        pl.semaphore_signal(
            barrier,
            inc=1,
            device_id=partner(plan, section, devices, code),
            device_id_type=MESH,
        )


def attend(query_ref, length_ref, cache_hbm, cache, by_head, latent_ref, cache_sem, start_loads):
    tokens, heads, _ = query_ref.shape
    latent_width = LANES * len(by_head)
    value_width = LANES
    score_scale = (value_width + query_ref.shape[2] - latent_width) ** (-0.5)
    fetches = []
    for token in range(tokens):
        fetch = pltpu.make_async_copy(cache_hbm.at[token], cache.at[token], cache_sem.at[token])
        fetch.start()
        fetches.append(fetch)
    position = lax.broadcasted_iota(jnp.int32, (heads, cache.shape[2]), 1)
    for token in range(tokens):
        fetches[token].wait()
        if token == 2:
            start_loads()
        scores = jnp.dot(query_ref[token], cache[token], preferred_element_type=jnp.float32)
        usable = position < length_ref[token]
        masked = jnp.where(usable, scores * score_scale, -1e30)
        highest = jnp.max(masked, axis=1, keepdims=True)
        expos = jnp.where(usable, jnp.exp(masked - highest), 0.0)
        weights = expos * (1.0 / jnp.sum(expos, axis=1, keepdims=True))
        mixed = lax.dot_general(
            weights.astype(jnp.bfloat16),
            cache[token, 0:latent_width, :],
            (((1,), (1,)), ((), ())),
            preferred_element_type=jnp.float32,
        )
        for part, lines in enumerate(by_head):
            columns = slice(part * LANES, (part + 1) * LANES)
            lines[pl.ds(token, heads, stride=tokens), :] = mixed[:, columns]
    dests, rows, _ = latent_ref.shape
    for part, lines in enumerate(by_head):
        columns = slice(part * LANES, (part + 1) * LANES)
        latent_ref[:, :, columns] = lines[...].reshape(dests, rows, LANES).astype(jnp.bfloat16)


def work(plan, widths, refs, buffers, loads):
    (
        latent_ref,
        residual_ref,
        gain_ref,
        expert_ref,
        level_ref,
        value_ref,
        out_ref,
        out_weight,
        gate,
        up,
        down,
        latents,
        left,
        stream,
        square,
        gate_sum,
        up_sum,
        act,
        pass_send,
        pass_recv,
        send_sem,
        recv_sem,
    ) = refs
    partial = buffers[:CHUNKS]
    landings = (buffers[CHUNKS : 2 * CHUNKS], None, buffers[2 * CHUNKS : 3 * CHUNKS])
    rows_of = buffers[3 * CHUNKS :]
    starts = [sum(widths[:k]) for k in range(CHUNKS)]
    section, me, devices = places()
    blocks, rows, halvings = plan.blocks, plan.rows, plan.halvings
    base = pl.ds(0, rows)
    owning = section < 3

    def peer(code):
        return partner(plan, section, devices, code)

    def when_owning(owns, run):
        if plan.core == 0:
            if owns:
                run()
        else:
            pl.when(owning if owns else jnp.logical_not(owning))(run)

    pl.semaphore_wait(pltpu.get_barrier_semaphore(), GROUP - 1)

    def passing(code):
        slot = code if plan.core == 0 else code // 2
        return pltpu.make_async_remote_copy(
            src_ref=latent_ref.at[devices[code]],
            dst_ref=latents.at[slot],
            send_sem=pass_send,
            recv_sem=pass_recv,
            device_id=peer(code),
            device_id_type=MESH,
        )

    def passed(slots):
        return pltpu.make_async_remote_copy(
            src_ref=latent_ref.at[slots],
            dst_ref=latents.at[slots],
            send_sem=pass_send,
            recv_sem=pass_recv,
            device_id=peer(1),
            device_id_type=MESH,
        )

    def pass_out():
        for code in range(1, GROUP):
            passing(code).start()
        latents[0] = latent_ref[me]
        passed(pl.ds(1, blocks - 1)).wait_recv()

    when_owning(True, pass_out)
    when_owning(False, lambda: passed(pl.ds(0, blocks)).wait_recv())
    for head in range(2):
        lines = latents[pl.ds(0, blocks), head * ROWS : (head + 1) * ROWS, :].astype(jnp.float32)
        lines = lines.reshape(rows, lines.shape[2]).astype(jnp.bfloat16)
        valued = jnp.dot(lines, value_ref[head], preferred_element_type=jnp.float32)
        left[base, head * LANES : (head + 1) * LANES] = valued.astype(jnp.bfloat16)

    def copy_of(source, target, phase, chunk, slot, code):
        return pltpu.make_async_remote_copy(
            src_ref=source,
            dst_ref=target,
            send_sem=send_sem.at[phase % 2, chunk],
            recv_sem=recv_sem.at[phase % 2, chunk, slot],
            device_id=peer(code),
            device_id_type=MESH,
        )

    def arrived(buffer, places, phase, chunk, slot):
        lines = buffer[chunk].at[places]
        copy_of(lines, lines, phase, chunk, slot, 1).wait_recv()

    def sent(buffer, phase, count):
        for chunk in range(CHUNKS):
            lines = buffer[chunk].at[pl.ds(0, count)]
            copy_of(lines, lines, phase, chunk, NEAR, 1).wait_send()

    def halving(phase, chunk, step):
        half = (blocks // 2) >> step
        places = pl.ds(half, half)
        return copy_of(
            partial[chunk].at[places],
            landings[phase][chunk].at[places],
            phase,
            chunk,
            HALVED + step,
            1 << plan.order(chunk)[step],
        )

    def sum_send(phase, chunk, step):
        if step < halvings:
            halving(phase, chunk, step).start()
            return

        def to_owners():
            for place in range(1, SPREAD):
                copy_of(
                    partial[chunk].at[place],
                    landings[phase][chunk].at[place],
                    phase,
                    chunk,
                    NEAR,
                    plan.code(chunk, place),
                ).start()

        def to_owners_across():
            for place in range(SPREAD):
                copy_of(
                    partial[chunk].at[place],
                    landings[phase][chunk].at[16 + place],
                    phase,
                    chunk,
                    FAR,
                    plan.code(chunk, place) + 1,
                ).start()

        when_owning(True, to_owners)
        when_owning(False, to_owners_across)

    def sum_sent(phase):
        when_owning(True, lambda: sent(partial, phase, blocks - 1))
        when_owning(False, lambda: sent(partial, phase, blocks))

    def add_rows(phase, chunk, half, first, count):
        @pl.loop(0, count)
        def _(i):
            row = first + i
            partial[chunk][row] = partial[chunk][row] + landings[phase][chunk][half + row]

    def sum_step(phase, chunk, step):
        half = (blocks // 2) >> step
        halving(phase, chunk, step).wait_recv()
        ahead = half // 2 if step < halvings - 1 else 0
        add_rows(phase, chunk, half, ahead, half - ahead)
        sum_send(phase, chunk, step + 1)
        if ahead:
            add_rows(phase, chunk, half, 0, ahead)

    def sum_last(phase, chunk):
        total = partial[chunk][0].astype(jnp.float32)
        arrived(landings[phase], pl.ds(1, SPREAD - 1), phase, chunk, NEAR)
        for place in range(1, SPREAD):
            total = total + landings[phase][chunk][place].astype(jnp.float32)
        if plan.core == 1:
            arrived(landings[phase], pl.ds(16, SPREAD), phase, chunk, FAR)
            for place in range(SPREAD):
                total = total + landings[phase][chunk][16 + place].astype(jnp.float32)
        return total

    def tiled(chunk, one):
        whole = widths[chunk] // TILE

        @pl.loop(0, whole)
        def _(i):
            one(pl.multiple_of(i * TILE, TILE), TILE)

        if widths[chunk] % TILE:
            one(whole * TILE, widths[chunk] % TILE)

    def project(chunk, operand, weight, scale):
        def one(offset, size):
            inner = pl.ds(offset, size)
            outer = pl.ds(pl.multiple_of(starts[chunk] + offset, LANES), size)
            product = jnp.dot(
                operand[base, :], weight[:, outer], preferred_element_type=jnp.float32
            )
            if scale is not None:
                product = product * scale
            for i, code in enumerate(plan.codes()):
                block = product[i * ROWS : (i + 1) * ROWS]
                partial[chunk][plan.place(chunk, code), :, inner] = block.astype(jnp.bfloat16)

        tiled(chunk, one)

    def gather(chunk, place, across):
        return copy_of(
            rows_of[chunk].at[0],
            rows_of[chunk].at[place],
            1,
            chunk,
            NEAR,
            plan.code(chunk, place) + across,
        )

    def doubling(chunk, step):
        count = (blocks // 2) >> step
        return copy_of(
            rows_of[chunk].at[pl.ds(0, count)],
            rows_of[chunk].at[pl.ds(count, count)],
            1,
            chunk,
            HALVED + step,
            1 << plan.order(chunk)[step],
        )

    def share_lanes():
        lane = lax.broadcasted_iota(jnp.int32, (ROWS, LANES), 1)
        own = lax.broadcasted_iota(jnp.int32, (ROWS, ROWS), 0) == lax.broadcasted_iota(
            jnp.int32, (ROWS, ROWS), 1
        )

        def column(ref, k):
            line = jnp.broadcast_to(ref[k : k + 1, :].astype(jnp.float32), (ROWS, ROWS))
            return jnp.sum(jnp.where(own, line, 0.0), axis=1, keepdims=True)

        levels = [column(level_ref, k) for k in range(TOPK)]
        named = jnp.where(lane < EXPERTS, lane, lane - EXPERTS).astype(jnp.float32)
        mixed = jnp.zeros((ROWS, LANES), jnp.float32)
        for k in range(TOPK):
            mixed += jnp.where(named == column(expert_ref, k), levels[k] / sum(levels), 0.0)
        coarse = mixed.astype(jnp.bfloat16).astype(jnp.float32)
        return lane, jnp.where(lane < EXPERTS, coarse, mixed - coarse)

    def attended_rows(chunk):
        columns = pl.ds(starts[chunk], widths[chunk])
        total = residual_ref[:, columns].astype(jnp.float32) + sum_last(0, chunk)
        total = total.astype(jnp.bfloat16)
        stream[:, columns] = total
        total = total.astype(jnp.float32)
        squares = total * total
        folded = sum(squares[:, i : i + LANES] for i in range(0, widths[chunk], LANES))
        square[...] = folded if chunk == 0 else square[...] + folded
        scaled = total * gain_ref[:, columns]
        rows_of[chunk][0, :, : widths[chunk]] = scaled.astype(jnp.bfloat16)
        if chunk == CHUNKS - 1:
            mean = jnp.sum(square[...], axis=1, keepdims=True) / stream.shape[1]
            level = lax.rsqrt(mean + 1e-06)
            coarse = level.astype(jnp.bfloat16).astype(jnp.float32)
            lane, extra = share_lanes()
            extra = jnp.where(lane == 2 * EXPERTS, coarse, extra)
            extra = jnp.where(lane == 2 * EXPERTS + 1, level - coarse, extra)
            rows_of[chunk][0, :, widths[chunk] :] = extra.astype(jnp.bfloat16)
        for place in range(SPREAD):
            if place:
                gather(chunk, place, 0).start()
            if plan.core == 1:
                gather(chunk, place, 1).start()

    def first_doubling(chunk):
        when_owning(True, lambda: arrived(rows_of, pl.ds(1, SPREAD - 1), 1, chunk, NEAR))
        when_owning(False, lambda: arrived(rows_of, pl.ds(0, SPREAD), 1, chunk, NEAR))
        doubling(chunk, halvings - 1).start()

    def stacked(chunk, columns):
        lines = [
            rows_of[chunk][plan.place(chunk, code), :, columns].astype(jnp.float32)
            for code in plan.codes()
        ]
        return jnp.concatenate(lines, axis=0)

    def hidden_sums(chunk):
        doubling(chunk, 0).wait_recv()

        def one(offset, size):
            outer = pl.ds(pl.multiple_of(starts[chunk] + offset, LANES), size)
            lines = stacked(chunk, pl.ds(offset, size)).astype(jnp.bfloat16)
            gate_sum[base, :] += jnp.dot(lines, gate[outer, :], preferred_element_type=jnp.float32)
            up_sum[base, :] += jnp.dot(lines, up[outer, :], preferred_element_type=jnp.float32)

        tiled(chunk, one)

    def staggered(count, stage):
        for time in range(count + LAG * (CHUNKS // DIMS - 1)):
            for group in range(CHUNKS // DIMS):
                if 0 <= time - LAG * group < count:
                    for chunk in range(group * DIMS, (group + 1) * DIMS):
                        stage(chunk, time - LAG * group)

    def until_hidden(chunk, step):
        if step == 0:
            project(chunk, left, out_weight, None)
            sum_send(0, chunk, 0)
        elif step <= halvings:
            sum_step(0, chunk, step - 1)
        elif step == halvings + 1:
            when_owning(True, functools.partial(attended_rows, chunk))
        elif step == halvings + 2:
            first_doubling(chunk)
        elif step <= 2 * halvings + 1:
            done = step - halvings - 2
            doubling(chunk, halvings - done).wait_recv()
            doubling(chunk, halvings - done - 1).start()
        else:
            hidden_sums(chunk)

    def until_output(chunk, step):
        if step == 0:
            project(chunk, act, down, share)
            sum_send(2, chunk, 0)
        elif step <= halvings:
            sum_step(2, chunk, step - 1)
        else:
            when_owning(True, functools.partial(result_rows, chunk))

    def result_rows(chunk):
        columns = pl.ds(starts[chunk], widths[chunk])
        result = stream[:, columns].astype(jnp.float32) + sum_last(2, chunk)
        out_ref[:, columns] = result.astype(jnp.bfloat16)

    gate_sum[base, :] = jnp.zeros((rows, gate_sum.shape[1]), jnp.float32)
    up_sum[base, :] = jnp.zeros((rows, up_sum.shape[1]), jnp.float32)
    for load in loads[:3]:
        load.wait()
    staggered(2 * halvings + 3, until_hidden)
    shares = stacked(CHUNKS - 1, pl.ds(widths[CHUNKS - 1], LANES))
    lane = lax.broadcasted_iota(jnp.int32, shares.shape, 1)
    expert = me // (GROUP // EXPERTS)

    def picked(first, second):
        chosen = (lane == first) | (lane == second)
        return jnp.sum(jnp.where(chosen, shares, 0.0), axis=1, keepdims=True)

    share = picked(expert, expert + EXPERTS)
    level = picked(2 * EXPERTS, 2 * EXPERTS + 1)
    hidden = gate_sum[base, :] * level
    hidden = hidden / (1.0 + jnp.exp(-hidden)) * (up_sum[base, :] * level)
    act[base, :] = hidden.astype(jnp.bfloat16)
    loads[3].wait()
    sum_sent(0)
    staggered(halvings + 2, until_output)

    def finish():
        passed(pl.ds(0, GROUP - 1)).wait_send()
        near = SPREAD - 1 if plan.core == 0 else 2 * SPREAD - 1
        sent(rows_of, 1, blocks - SPREAD + near)

    def blank():
        out_ref[...] = jnp.zeros_like(out_ref)
        sent(rows_of, 1, blocks - SPREAD)

    when_owning(True, finish)
    when_owning(False, blank)
    sum_sent(2)


def layer_kernel(
    widths,
    length_ref,
    query_ref,
    residual_ref,
    gain_ref,
    expert_ref,
    level_ref,
    value_ref,
    cache_hbm,
    out_weight_hbm,
    gate_hbm,
    up_hbm,
    down_hbm,
    out_ref,
    out_weight,
    gate,
    up,
    down,
    cache,
    latent_ref,
    latents,
    left,
    stream,
    square,
    gate_sum,
    up_sum,
    act,
    cache_sem,
    load_sem,
    pass_send,
    pass_recv,
    send_sem,
    recv_sem,
    *buffers,
):
    parts = latent_ref.shape[2] // LANES
    by_head, buffers = buffers[:parts], buffers[parts:]
    loads = [
        pltpu.make_async_copy(source, target, load_sem.at[i])
        for i, (source, target) in enumerate(
            ((out_weight_hbm, out_weight), (gate_hbm, gate), (up_hbm, up), (down_hbm, down))
        )
    ]
    refs = (latent_ref, residual_ref, gain_ref, expert_ref, level_ref, value_ref, out_ref)
    refs += (out_weight, gate, up, down, latents, left, stream, square, gate_sum, up_sum, act)
    refs += (pass_send, pass_recv, send_sem, recv_sem)
    section = lax.axis_index("sec")
    core = section % 2
    for number in range(2):
        pl.when(core == number)(functools.partial(greet, Plan(number)))

    def start_loads():
        for load in loads:
            load.start()

    pl.when(section < 3)(
        lambda: attend(
            query_ref, length_ref, cache_hbm, cache, by_head, latent_ref, cache_sem, start_loads
        )
    )
    pl.when(section == 3)(start_loads)
    for number in range(2):
        pl.when(core == number)(
            functools.partial(work, Plan(number), widths, refs, buffers, loads)
        )


def layer(lengths, queries, residual, gain, experts, levels, value_up, cache, *weights):
    width = residual.shape[1]
    widths = [LANES * units for _, _, units in TABLE]
    hidden = weights[1].shape[1]
    tokens, heads, _ = queries.shape
    latent_width = value_up.shape[1]
    bf16, f32 = jnp.bfloat16, jnp.float32
    vmem = pl.BlockSpec(memory_space=pltpu.VMEM)
    hbm = pl.BlockSpec(memory_space=pl.ANY)
    latents = pltpu.VMEM((GROUP, heads * tokens // GROUP, latent_width), bf16)
    scratch = [pltpu.VMEM(weight.shape, bf16) for weight in weights]
    scratch += [
        pltpu.VMEM(cache.shape, bf16),
        latents,
        latents,
        pltpu.VMEM((GROUP * ROWS, 2 * LANES), bf16),
        pltpu.VMEM((ROWS, width), bf16),
        pltpu.VMEM((ROWS, LANES), f32),
        pltpu.VMEM((GROUP * ROWS, hidden), f32),
        pltpu.VMEM((GROUP * ROWS, hidden), f32),
        pltpu.VMEM((GROUP * ROWS, hidden), bf16),
        pltpu.SemaphoreType.DMA((tokens,)),
        pltpu.SemaphoreType.DMA((4,)),
        pltpu.SemaphoreType.DMA,
        pltpu.SemaphoreType.DMA,
        pltpu.SemaphoreType.DMA((2, CHUNKS)),
        pltpu.SemaphoreType.DMA((2, CHUNKS, SLOTS)),
    ]
    scratch += [pltpu.VMEM((heads * tokens, LANES), f32)] * (latent_width // LANES)
    scratch += [pltpu.VMEM((GROUP, ROWS, w), bf16) for w in widths] * 3
    extra = [0] * (CHUNKS - 1) + [LANES]
    scratch += [pltpu.VMEM((GROUP, ROWS, w + e), bf16) for w, e in zip(widths, extra)]
    return pl.pallas_call(
        functools.partial(layer_kernel, widths),
        out_shape=jax.ShapeDtypeStruct(residual.shape, bf16),
        in_specs=[pl.BlockSpec(memory_space=pltpu.SMEM)] + [vmem] * 6 + [hbm] * 5,
        out_specs=vmem,
        scratch_shapes=scratch,
        compiler_params=pltpu.CompilerParams(
            collective_id=0, has_side_effects=True, vmem_limit_bytes=58 * 1024 * 1024
        ),
    )(lengths, queries, residual, gain, experts, levels, value_up, cache, *weights)


def body(
    queries,
    latent_cache,
    cache_length,
    residual,
    norm_gain,
    value_up,
    out_weight,
    gate_weight,
    up_weight,
    down_weight,
    expert_index,
    gate_level,
):
    return layer(
        cache_length,
        queries,
        residual,
        norm_gain.reshape(1, -1),
        expert_index.T,
        gate_level.T,
        value_up,
        jnp.swapaxes(latent_cache, 1, 2),
        out_weight,
        gate_weight,
        up_weight,
        down_weight,
    )


def solution(mesh):
    placed = (
        P(("sec", "dev"), None, None),
        P(("sec", "dev"), None, None),
        P(("sec", "dev")),
        P(("sec", "dev"), None),
        P(),
        P("dev", None, None),
        P("dev", None),
        P(None, "dev"),
        P(None, "dev"),
        P("dev", None),
        P(("sec", "dev"), None),
        P(("sec", "dev"), None),
    )
    return jax.shard_map(
        body, mesh=mesh, in_specs=placed, out_specs=P(("sec", "dev"), None), check_vma=False
    )
```

```python
import functools

import jax
import jax.numpy as jnp
from jax import lax
from jax.experimental import pallas as pl
from jax.experimental.pallas import tpu as pltpu
from jax.sharding import PartitionSpec as P

EXPERTS = 4
TOPK = 2
ROWS = 8
GROUP = 32
DIMS = 5
LANES = 128
TABLE = (
    ((0, 1, 2, 3, 4), 0, 3),
    ((1, 2, 3, 4, 0), 1, 3),
    ((2, 3, 4, 0, 1), 2, 3),
    ((3, 4, 0, 1, 2), 3, 3),
    ((4, 0, 1, 2, 3), 0, 3),
    ((0, 1, 2, 3, 4), 1, 3),
    ((1, 2, 3, 4, 0), 2, 3),
    ((2, 3, 4, 0, 1), 3, 3),
    ((3, 4, 0, 1, 2), 0, 3),
    ((4, 0, 1, 2, 3), 1, 3),
    ((0, 1, 2, 3, 4), 2, 3),
    ((1, 2, 3, 4, 0), 3, 3),
    ((2, 3, 4, 0, 1), 0, 3),
    ((3, 4, 0, 1, 2), 1, 3),
    ((4, 0, 1, 2, 3), 2, 3),
    ((0, 1, 2, 3, 4), 3, 3),
    ((1, 2, 3, 4, 0), 0, 2),
    ((2, 3, 4, 0, 1), 1, 2),
    ((3, 4, 0, 1, 2), 2, 2),
    ((4, 0, 1, 2, 3), 3, 2),
)
LAG = 0
CHUNKS = len(TABLE)
SPREAD = 4
NEAR, HALVED, FAR = 0, 1, 3
SLOTS = 4
MASKS = (1, 2, 6, 8, 24)
MESH = pl.DeviceIdType.MESH


def mask_of(code):
    mask = 0
    for dim in range(DIMS):
        if (code >> dim) & 1:
            mask ^= MASKS[dim]
    return mask


def flipped(bits, mask):
    total = 0
    for i, bit in enumerate(bits):
        total = total + (1 << i) * ((1 - bit) if (mask >> i) & 1 else bit)
    return total


class Plan:
    def __init__(self, core):
        self.core = core
        self.blocks = GROUP if core == 0 else GROUP // 2
        self.halvings = 3 if core == 0 else 2
        self.rows = self.blocks * ROWS

    def order(self, chunk):
        if self.core == 0:
            return TABLE[chunk][0]
        return [1 + (TABLE[chunk][1] + i) % 4 for i in range(4)]

    def codes(self):
        return [(code if self.core == 0 else 2 * code) for code in range(self.blocks)]

    def place(self, chunk, code):
        order = self.order(chunk)
        place = 0
        for step, dim in enumerate(order):
            place += ((code >> dim) & 1) << (len(order) - 1 - step)
        return place

    def code(self, chunk, place):
        order = self.order(chunk)
        code = 0
        for step, dim in enumerate(order):
            code += ((place >> (len(order) - 1 - step)) & 1) << dim
        return code


def places():
    section = lax.axis_index("sec")
    me = lax.axis_index("dev")
    bits = [(me // (1 << i)) % 2 for i in range(DIMS)]
    devices = {code: flipped(bits, mask_of(code)) for code in range(GROUP)}
    return section, me, devices


def partner(plan, section, devices, code):
    across = lax.rem(section + 2, 4)
    return (across if plan.core == 1 and code % 2 else section, devices[code])


def greet(plan):
    section, _, devices = places()
    barrier = pltpu.get_barrier_semaphore()
    for code in range(1, GROUP):
        pl.semaphore_signal(
            barrier,
            inc=1,
            device_id=partner(plan, section, devices, code),
            device_id_type=MESH,
        )


def attend(
    query_hbm,
    query_ref,
    length_ref,
    cache_hbm,
    cache,
    by_head,
    latent_ref,
    cache_sem,
    start_loads,
):
    tokens, heads, _ = query_ref.shape
    latent_width = LANES * len(by_head)
    value_width = LANES
    score_scale = (value_width + query_ref.shape[2] - latent_width) ** (-0.5)
    query_fetch = pltpu.make_async_copy(query_hbm, query_ref, cache_sem.at[tokens])
    query_fetch.start()
    fetches = []
    for token in range(tokens):
        fetch = pltpu.make_async_copy(cache_hbm.at[token], cache.at[token], cache_sem.at[token])
        fetch.start()
        fetches.append(fetch)
    query_fetch.wait()
    position = lax.broadcasted_iota(jnp.int32, (heads, cache.shape[2]), 1)
    for token in range(tokens):
        fetches[token].wait()
        if token == 2:
            start_loads()
        scores = jnp.dot(query_ref[token], cache[token], preferred_element_type=jnp.float32)
        usable = position < length_ref[token]
        masked = jnp.where(usable, scores * score_scale, -1e30)
        highest = jnp.max(masked, axis=1, keepdims=True)
        expos = jnp.where(usable, jnp.exp(masked - highest), 0.0)
        weights = expos * (1.0 / jnp.sum(expos, axis=1, keepdims=True))
        mixed = lax.dot_general(
            weights.astype(jnp.bfloat16),
            cache[token, 0:latent_width, :],
            (((1,), (1,)), ((), ())),
            preferred_element_type=jnp.float32,
        )
        for part, lines in enumerate(by_head):
            columns = slice(part * LANES, (part + 1) * LANES)
            lines[pl.ds(token, heads, stride=tokens), :] = mixed[:, columns]
    dests, rows, _ = latent_ref.shape
    for part, lines in enumerate(by_head):
        columns = slice(part * LANES, (part + 1) * LANES)
        latent_ref[:, :, columns] = lines[...].reshape(dests, rows, LANES).astype(jnp.bfloat16)


def work(plan, widths, refs, buffers, loads):
    (
        latent_ref,
        residual_ref,
        gain_ref,
        expert_ref,
        level_ref,
        value_ref,
        out_ref,
        out_weight,
        gate,
        up,
        down,
        latents,
        left,
        stream,
        square,
        gate_sum,
        up_sum,
        act,
        pass_send,
        pass_recv,
        send_sem,
        recv_sem,
    ) = refs
    partial = buffers[:CHUNKS]
    landings = (buffers[CHUNKS : 2 * CHUNKS], None, buffers[2 * CHUNKS : 3 * CHUNKS])
    rows_of = buffers[3 * CHUNKS :]
    starts = [sum(widths[:k]) for k in range(CHUNKS)]
    section, me, devices = places()
    blocks, rows, halvings = plan.blocks, plan.rows, plan.halvings
    base = pl.ds(0, rows)
    owning = section < 3

    def peer(code):
        return partner(plan, section, devices, code)

    def when_owning(owns, run):
        if plan.core == 0:
            if owns:
                run()
        else:
            pl.when(owning if owns else jnp.logical_not(owning))(run)

    pl.semaphore_wait(pltpu.get_barrier_semaphore(), GROUP - 1)

    def passing(code):
        slot = code if plan.core == 0 else code // 2
        return pltpu.make_async_remote_copy(
            src_ref=latent_ref.at[devices[code]],
            dst_ref=latents.at[slot],
            send_sem=pass_send,
            recv_sem=pass_recv,
            device_id=peer(code),
            device_id_type=MESH,
        )

    def passed(slots):
        return pltpu.make_async_remote_copy(
            src_ref=latent_ref.at[slots],
            dst_ref=latents.at[slots],
            send_sem=pass_send,
            recv_sem=pass_recv,
            device_id=peer(1),
            device_id_type=MESH,
        )

    def pass_out():
        for code in range(1, GROUP):
            passing(code).start()
        latents[0] = latent_ref[me]
        passed(pl.ds(1, blocks - 1)).wait_recv()

    when_owning(True, pass_out)
    when_owning(False, lambda: passed(pl.ds(0, blocks)).wait_recv())
    loads[0].wait()
    for head in range(2):
        lines = latents[pl.ds(0, blocks), head * ROWS : (head + 1) * ROWS, :].astype(jnp.float32)
        lines = lines.reshape(rows, lines.shape[2]).astype(jnp.bfloat16)
        valued = jnp.dot(lines, value_ref[head], preferred_element_type=jnp.float32)
        left[base, head * LANES : (head + 1) * LANES] = valued.astype(jnp.bfloat16)

    def copy_of(source, target, phase, chunk, slot, code):
        return pltpu.make_async_remote_copy(
            src_ref=source,
            dst_ref=target,
            send_sem=send_sem.at[phase % 2, chunk],
            recv_sem=recv_sem.at[phase % 2, chunk, slot],
            device_id=peer(code),
            device_id_type=MESH,
        )

    def arrived(buffer, places, phase, chunk, slot):
        lines = buffer[chunk].at[places]
        copy_of(lines, lines, phase, chunk, slot, 1).wait_recv()

    def sent(buffer, phase, count):
        for chunk in range(CHUNKS):
            lines = buffer[chunk].at[pl.ds(0, count)]
            copy_of(lines, lines, phase, chunk, NEAR, 1).wait_send()

    def halving(phase, chunk, step):
        half = (blocks // 2) >> step
        places = pl.ds(half, half)
        return copy_of(
            partial[chunk].at[places],
            landings[phase][chunk].at[places],
            phase,
            chunk,
            HALVED + step,
            1 << plan.order(chunk)[step],
        )

    def sum_send(phase, chunk, step):
        if step < halvings:
            halving(phase, chunk, step).start()
            return

        def to_owners():
            for place in range(1, SPREAD):
                copy_of(
                    partial[chunk].at[place],
                    landings[phase][chunk].at[place],
                    phase,
                    chunk,
                    NEAR,
                    plan.code(chunk, place),
                ).start()

        def to_owners_across():
            for place in range(SPREAD):
                copy_of(
                    partial[chunk].at[place],
                    landings[phase][chunk].at[16 + place],
                    phase,
                    chunk,
                    FAR,
                    plan.code(chunk, place) + 1,
                ).start()

        when_owning(True, to_owners)
        when_owning(False, to_owners_across)

    def sum_sent(phase):
        when_owning(True, lambda: sent(partial, phase, blocks - 1))
        when_owning(False, lambda: sent(partial, phase, blocks))

    def add_rows(phase, chunk, half, first, count):
        @pl.loop(0, count)
        def _(i):
            row = first + i
            partial[chunk][row] = partial[chunk][row] + landings[phase][chunk][half + row]

    def sum_step(phase, chunk, step):
        half = (blocks // 2) >> step
        halving(phase, chunk, step).wait_recv()
        ahead = half // 2 if step < halvings - 1 else 0
        add_rows(phase, chunk, half, ahead, half - ahead)
        sum_send(phase, chunk, step + 1)
        if ahead:
            add_rows(phase, chunk, half, 0, ahead)

    def sum_last(phase, chunk):
        total = partial[chunk][0].astype(jnp.float32)
        arrived(landings[phase], pl.ds(1, SPREAD - 1), phase, chunk, NEAR)
        for place in range(1, SPREAD):
            total = total + landings[phase][chunk][place].astype(jnp.float32)
        if plan.core == 1:
            arrived(landings[phase], pl.ds(16, SPREAD), phase, chunk, FAR)
            for place in range(SPREAD):
                total = total + landings[phase][chunk][16 + place].astype(jnp.float32)
        return total

    def project(chunk, operand, weight, scale):
        columns = pl.ds(starts[chunk], widths[chunk])
        product = jnp.dot(operand[base, :], weight[:, columns], preferred_element_type=jnp.float32)
        if scale is not None:
            product = product * scale
        for i, code in enumerate(plan.codes()):
            block = product[i * ROWS : (i + 1) * ROWS]
            partial[chunk][plan.place(chunk, code)] = block.astype(jnp.bfloat16)

    def gather(chunk, place, across):
        return copy_of(
            rows_of[chunk].at[0],
            rows_of[chunk].at[place],
            1,
            chunk,
            NEAR,
            plan.code(chunk, place) + across,
        )

    def doubling(chunk, step):
        count = (blocks // 2) >> step
        return copy_of(
            rows_of[chunk].at[pl.ds(0, count)],
            rows_of[chunk].at[pl.ds(count, count)],
            1,
            chunk,
            HALVED + step,
            1 << plan.order(chunk)[step],
        )

    def share_lanes():
        lane = lax.broadcasted_iota(jnp.int32, (ROWS, LANES), 1)
        own = lax.broadcasted_iota(jnp.int32, (ROWS, ROWS), 0) == lax.broadcasted_iota(
            jnp.int32, (ROWS, ROWS), 1
        )

        def column(ref, k):
            line = jnp.broadcast_to(ref[k : k + 1, :].astype(jnp.float32), (ROWS, ROWS))
            return jnp.sum(jnp.where(own, line, 0.0), axis=1, keepdims=True)

        levels = [column(level_ref, k) for k in range(TOPK)]
        named = jnp.where(lane < EXPERTS, lane, lane - EXPERTS).astype(jnp.float32)
        mixed = jnp.zeros((ROWS, LANES), jnp.float32)
        for k in range(TOPK):
            mixed += jnp.where(named == column(expert_ref, k), levels[k] / sum(levels), 0.0)
        coarse = mixed.astype(jnp.bfloat16).astype(jnp.float32)
        return lane, jnp.where(lane < EXPERTS, coarse, mixed - coarse)

    def attended_rows(chunk):
        columns = pl.ds(starts[chunk], widths[chunk])
        total = residual_ref[:, columns].astype(jnp.float32) + sum_last(0, chunk)
        total = total.astype(jnp.bfloat16)
        stream[:, columns] = total
        total = total.astype(jnp.float32)
        squares = total * total
        folded = sum(squares[:, i : i + LANES] for i in range(0, widths[chunk], LANES))
        square[...] = folded if chunk == 0 else square[...] + folded
        scaled = total * gain_ref[:, columns]
        rows_of[chunk][0, :, : widths[chunk]] = scaled.astype(jnp.bfloat16)
        if chunk == CHUNKS - 1:
            mean = jnp.sum(square[...], axis=1, keepdims=True) / stream.shape[1]
            level = lax.rsqrt(mean + 1e-06)
            coarse = level.astype(jnp.bfloat16).astype(jnp.float32)
            lane, extra = share_lanes()
            extra = jnp.where(lane == 2 * EXPERTS, coarse, extra)
            extra = jnp.where(lane == 2 * EXPERTS + 1, level - coarse, extra)
            rows_of[chunk][0, :, widths[chunk] :] = extra.astype(jnp.bfloat16)
        for place in range(SPREAD):
            if place:
                gather(chunk, place, 0).start()
            if plan.core == 1:
                gather(chunk, place, 1).start()

    def first_doubling(chunk):
        when_owning(True, lambda: arrived(rows_of, pl.ds(1, SPREAD - 1), 1, chunk, NEAR))
        when_owning(False, lambda: arrived(rows_of, pl.ds(0, SPREAD), 1, chunk, NEAR))
        doubling(chunk, halvings - 1).start()

    def stacked(chunk, columns):
        lines = [
            rows_of[chunk][plan.place(chunk, code), :, columns].astype(jnp.float32)
            for code in plan.codes()
        ]
        return jnp.concatenate(lines, axis=0)

    def hidden_sums(chunk):
        doubling(chunk, 0).wait_recv()

        columns = pl.ds(starts[chunk], widths[chunk])
        lines = stacked(chunk, pl.ds(0, widths[chunk])).astype(jnp.bfloat16)
        gate_sum[base, :] += jnp.dot(lines, gate[columns, :], preferred_element_type=jnp.float32)
        up_sum[base, :] += jnp.dot(lines, up[columns, :], preferred_element_type=jnp.float32)

    def staggered(count, stage):
        for time in range(count + LAG * (CHUNKS // DIMS - 1)):
            for group in range(CHUNKS // DIMS):
                if 0 <= time - LAG * group < count:
                    for chunk in range(group * DIMS, (group + 1) * DIMS):
                        stage(chunk, time - LAG * group)

    def until_hidden(chunk, step):
        if step == 0:
            project(chunk, left, out_weight, None)
            sum_send(0, chunk, 0)
        elif step <= halvings:
            sum_step(0, chunk, step - 1)
        elif step == halvings + 1:
            when_owning(True, functools.partial(attended_rows, chunk))
        elif step == halvings + 2:
            first_doubling(chunk)
        elif step <= 2 * halvings + 1:
            done = step - halvings - 2
            doubling(chunk, halvings - done).wait_recv()
            doubling(chunk, halvings - done - 1).start()
        else:
            hidden_sums(chunk)

    def until_output(chunk, step):
        if step == 0:
            project(chunk, act, down, share)
            sum_send(2, chunk, 0)
        elif step <= halvings:
            sum_step(2, chunk, step - 1)
        else:
            when_owning(True, functools.partial(result_rows, chunk))

    def result_rows(chunk):
        columns = pl.ds(starts[chunk], widths[chunk])
        result = stream[:, columns].astype(jnp.float32) + sum_last(2, chunk)
        out_ref[:, columns] = result.astype(jnp.bfloat16)

    gate_sum[base, :] = jnp.zeros((rows, gate_sum.shape[1]), jnp.float32)
    up_sum[base, :] = jnp.zeros((rows, up_sum.shape[1]), jnp.float32)
    for load in loads[1:6]:
        load.wait()
    staggered(2 * halvings + 3, until_hidden)
    shares = stacked(CHUNKS - 1, pl.ds(widths[CHUNKS - 1], LANES))
    lane = lax.broadcasted_iota(jnp.int32, shares.shape, 1)
    expert = me // (GROUP // EXPERTS)

    def picked(first, second):
        chosen = (lane == first) | (lane == second)
        return jnp.sum(jnp.where(chosen, shares, 0.0), axis=1, keepdims=True)

    share = picked(expert, expert + EXPERTS)
    level = picked(2 * EXPERTS, 2 * EXPERTS + 1)
    hidden = gate_sum[base, :] * level
    hidden = hidden / (1.0 + jnp.exp(-hidden)) * (up_sum[base, :] * level)
    act[base, :] = hidden.astype(jnp.bfloat16)
    loads[6].wait()
    sum_sent(0)
    staggered(halvings + 2, until_output)

    def finish():
        passed(pl.ds(0, GROUP - 1)).wait_send()
        near = SPREAD - 1 if plan.core == 0 else 2 * SPREAD - 1
        sent(rows_of, 1, blocks - SPREAD + near)

    def blank():
        out_ref[...] = jnp.zeros_like(out_ref)
        sent(rows_of, 1, blocks - SPREAD)

    when_owning(True, finish)
    when_owning(False, blank)
    sum_sent(2)


def layer_kernel(
    widths,
    length_ref,
    expert_ref,
    level_ref,
    query_hbm,
    cache_hbm,
    value_hbm,
    residual_hbm,
    gain_hbm,
    out_weight_hbm,
    gate_hbm,
    up_hbm,
    down_hbm,
    out_ref,
    query_ref,
    cache,
    value_ref,
    residual_ref,
    gain_ref,
    out_weight,
    gate,
    up,
    down,
    latent_ref,
    latents,
    left,
    stream,
    square,
    gate_sum,
    up_sum,
    act,
    cache_sem,
    load_sem,
    pass_send,
    pass_recv,
    send_sem,
    recv_sem,
    *buffers,
):
    parts = latent_ref.shape[2] // LANES
    by_head, buffers = buffers[:parts], buffers[parts:]
    loads = [
        pltpu.make_async_copy(source, target, load_sem.at[i])
        for i, (source, target) in enumerate(
            (
                (value_hbm, value_ref),
                (residual_hbm, residual_ref),
                (gain_hbm, gain_ref),
                (out_weight_hbm, out_weight),
                (gate_hbm, gate),
                (up_hbm, up),
                (down_hbm, down),
            )
        )
    ]
    refs = (latent_ref, residual_ref, gain_ref, expert_ref, level_ref, value_ref, out_ref)
    refs += (out_weight, gate, up, down, latents, left, stream, square, gate_sum, up_sum, act)
    refs += (pass_send, pass_recv, send_sem, recv_sem)
    section = lax.axis_index("sec")
    core = section % 2
    for number in range(2):
        pl.when(core == number)(functools.partial(greet, Plan(number)))

    def start_loads():
        for load in loads:
            load.start()

    pl.when(section < 3)(
        lambda: attend(
            query_hbm,
            query_ref,
            length_ref,
            cache_hbm,
            cache,
            by_head,
            latent_ref,
            cache_sem,
            start_loads,
        )
    )
    pl.when(section == 3)(start_loads)
    for number in range(2):
        pl.when(core == number)(
            functools.partial(work, Plan(number), widths, refs, buffers, loads)
        )


def layer(lengths, experts, levels, queries, cache, *weights):
    value_up, residual = weights[:2]
    width = residual.shape[1]
    widths = [LANES * units for _, _, units in TABLE]
    hidden = weights[4].shape[1]
    tokens, heads, _ = queries.shape
    latent_width = value_up.shape[1]
    bf16, f32 = jnp.bfloat16, jnp.float32
    vmem = pl.BlockSpec(memory_space=pltpu.VMEM)
    hbm = pl.BlockSpec(memory_space=pl.ANY)
    latents = pltpu.VMEM((GROUP, heads * tokens // GROUP, latent_width), bf16)
    scratch = [pltpu.VMEM(array.shape, array.dtype) for array in (queries, cache, *weights)]
    scratch += [
        latents,
        latents,
        pltpu.VMEM((GROUP * ROWS, 2 * LANES), bf16),
        pltpu.VMEM((ROWS, width), bf16),
        pltpu.VMEM((ROWS, LANES), f32),
        pltpu.VMEM((GROUP * ROWS, hidden), f32),
        pltpu.VMEM((GROUP * ROWS, hidden), f32),
        pltpu.VMEM((GROUP * ROWS, hidden), bf16),
        pltpu.SemaphoreType.DMA((tokens + 1,)),
        pltpu.SemaphoreType.DMA((len(weights),)),
        pltpu.SemaphoreType.DMA,
        pltpu.SemaphoreType.DMA,
        pltpu.SemaphoreType.DMA((2, CHUNKS)),
        pltpu.SemaphoreType.DMA((2, CHUNKS, SLOTS)),
    ]
    scratch += [pltpu.VMEM((heads * tokens, LANES), f32)] * (latent_width // LANES)
    scratch += [pltpu.VMEM((GROUP, ROWS, w), bf16) for w in widths] * 3
    extra = [0] * (CHUNKS - 1) + [LANES]
    scratch += [pltpu.VMEM((GROUP, ROWS, w + e), bf16) for w, e in zip(widths, extra)]
    return pl.pallas_call(
        functools.partial(layer_kernel, widths),
        out_shape=jax.ShapeDtypeStruct(residual.shape, bf16),
        in_specs=[pl.BlockSpec(memory_space=pltpu.SMEM)] + [vmem] * 2 + [hbm] * 9,
        out_specs=vmem,
        scratch_shapes=scratch,
        compiler_params=pltpu.CompilerParams(
            collective_id=0, has_side_effects=True, vmem_limit_bytes=58 * 1024 * 1024
        ),
    )(lengths, experts, levels, queries, cache, *weights)


def body(
    queries,
    latent_cache,
    cache_length,
    residual,
    norm_gain,
    value_up,
    out_weight,
    gate_weight,
    up_weight,
    down_weight,
    expert_index,
    gate_level,
):
    return layer(
        cache_length,
        expert_index.T,
        gate_level.T,
        queries,
        jnp.swapaxes(latent_cache, 1, 2),
        value_up,
        residual,
        norm_gain.reshape(1, -1),
        out_weight,
        gate_weight,
        up_weight,
        down_weight,
    )


def solution(mesh):
    placed = (
        P(("sec", "dev"), None, None),
        P(("sec", "dev"), None, None),
        P(("sec", "dev")),
        P(("sec", "dev"), None),
        P(),
        P("dev", None, None),
        P("dev", None),
        P(None, "dev"),
        P(None, "dev"),
        P("dev", None),
        P(("sec", "dev"), None),
        P(("sec", "dev"), None),
    )
    return jax.shard_map(
        body, mesh=mesh, in_specs=placed, out_specs=P(("sec", "dev"), None), check_vma=False
    )
```
